256 devices in a mesh: samples: 64 (over z, y, x_hi), params: 4 (over x_lo, core).
Axes of the slice: x: 4 (x_hi: 2, x_lo: 2; x = x_hi * 2 + x_lo), y: 4, z: 8, core: 2. Of those that a mesh axis runs over, the one named last changes fastest.
Arguments:
- occupations: int32 [4096, 152], P('samples'), may hold values from 0 to 1, as said below
- connection_counts: int32 [4096], P('samples'), may hold values from 0 to 3072, as said below
- connection_orbitals: int32 [4, 196608], P(None, ('samples', 'params')), may hold values from 0 to 151, as said below
- connection_elements: float32 [2, 196608], P(None, ('samples', 'params')), may hold values from -2 to 2
- laser_step: int32 [], replicated, may hold values from 0 to 3999
- first_weight: bfloat16 [152, 1024], replicated, may hold values from -4 to 4
- first_bias: float32 [1024], replicated, may hold values from -3 to 3
- second_weight: bfloat16 [1024, 256], P('params'), may hold values from -1.25 to 1.25
- readout: float32 [2, 256], replicated, may hold values from -0.375 to 0.375
Outputs:
- local_energy: float32 [2, 4096], P(None, 'samples')
- change: float32 [2, 4096], P(None, 'samples')
The draws below stay inside these ranges and needn't reach their ends.
Inputs may be any that keep to these rules, and one draw needn't show every extreme that they name: `occupations`: each row has exactly 76 ones. `connection_counts`: the connections of block b of 64 consecutive samples fill the first slots q of that block in order of sample; the counts of a block sum to at most 3072, and to exactly 3072 in some block. `connection_orbitals`: the 4 orbitals of a slot are distinct; unused slots hold arbitrary orbitals in the range.
All inputs are finite; a program needn't handle non-finite values.
Results may differ from the reference program's by a relative error of at most 0.0099.
Values may be sent and summed in bfloat16 or wider, within the bound.
A program may use at most 64 MiB of HBM per device.

```python
import jax
import jax.numpy as jnp
from jax import lax

SO = 152
NEL = 76
HID = 1024
HID2 = 256
UPD = 4
ITERS = 2
S_DEV = 64
CAP = 768
SAMPLES = 4096
GSLOTS = 3072
SLOTS = 196608
N_PARAMS = 4


def draw_occupations(key, part):
    keys = jax.random.split(jax.random.fold_in(key, 11), SAMPLES)
    orders = jax.vmap(lambda single: jax.random.permutation(single, SO))(keys)
    return (orders < NEL).astype(jnp.int32)


def draw_connection_counts(key, part):
    blocks = SAMPLES // S_DEV
    first_key, second_key, third_key = jax.random.split(jax.random.fold_in(key, 23), 3)
    totals = jax.random.randint(first_key, (blocks,), GSLOTS // 4, GSLOTS + 1)
    fullest = jax.random.randint(second_key, (), 0, blocks)
    is_fullest = jnp.arange(blocks) == fullest
    totals = jnp.where(is_fullest, GSLOTS, totals).astype(jnp.int32)
    cuts = jax.random.randint(third_key, (blocks, S_DEV - 1), 0, totals[:, None] + 1)
    cuts = jnp.sort(cuts, axis=1).astype(jnp.int32)
    cuts = jnp.where(is_fullest[:, None], GSLOTS, cuts).astype(jnp.int32)
    bounds = jnp.concatenate([jnp.zeros((blocks, 1), jnp.int32), cuts, totals[:, None]], axis=1)
    return (bounds[:, 1:] - bounds[:, :-1]).reshape(-1).astype(jnp.int32)


def draw_connection_orbitals(key, part):
    first_key, second_key = jax.random.split(jax.random.fold_in(key, 37), 2)
    anchor = jax.random.randint(first_key, (1, SLOTS), 0, SO)
    stride = jax.random.randint(second_key, (1, SLOTS), 1, SO // UPD)
    offsets = jnp.arange(UPD, dtype=jnp.int32)[:, None]
    return ((anchor + offsets * stride) % SO).astype(jnp.int32)


def shard_levels(key, dims, shards, smallest, largest):
    gain, own = 1.0, jax.random.fold_in(key, 6)
    for position, parts in shards:
        draws = jnp.exp(jax.random.uniform(jax.random.fold_in(own, position), (parts,), jnp.float32, smallest / len(shards), largest / len(shards)))
        gain = gain * jnp.repeat(draws, dims[position] // parts).reshape([-1 if axis == position else 1 for axis in range(len(dims))])
    return gain


def normal_values(key, shape, scale, limit, cuts=(), held_as=jnp.bfloat16):
    level = shard_levels(key, shape, cuts, -0.22, 0.18) if cuts else 1.0
    entries = jax.random.normal(key, shape, jnp.float32) * scale * level
    return jnp.minimum(jnp.maximum(entries, -limit), limit).astype(held_as)


def setup_inputs(seed: int = 0) -> dict:
    seeds = jax.random.split(jax.random.key(seed), 10)
    occupations = draw_occupations(jax.random.fold_in(seeds[9], 71), 0)
    connection_counts = draw_connection_counts(jax.random.fold_in(seeds[9], 71), 0)
    connection_orbitals = draw_connection_orbitals(jax.random.fold_in(seeds[9], 71), 0)
    connection_elements = normal_values(seeds[3], (2, SLOTS), 0.15, 2.0, ((1, 256),), jnp.float32)
    laser_step = jax.random.randint(seeds[4], (), 0, 4000).astype(jnp.int32)
    first_weight = normal_values(seeds[5], (SO, HID), (2.6 * NEL ** -0.5), 4.0)
    first_bias = normal_values(seeds[6], (HID,), 0.5, 3.0, (), jnp.float32)
    second_weight = normal_values(seeds[7], (HID, HID2), (2.6 * HID ** -0.5), 1.25, ((0, 4),))
    readout = normal_values(seeds[8], (2, HID2), HID2 ** -0.5, 0.375, (), jnp.float32)
    return dict(occupations=occupations, connection_counts=connection_counts, connection_orbitals=connection_orbitals, connection_elements=connection_elements, laser_step=laser_step, first_weight=first_weight, first_bias=first_bias, second_weight=second_weight, readout=readout)


PRECISE = lax.Precision.HIGHEST
FIELD_SCALE = 0.8
FIELD_RATE = 0.0123
DIAG_SHIFT = 0.01


def slot_values(base_pre, orbitals, deltas, first_weight, second_weight, readout):
    columns = jnp.arange(first_weight.shape[0], dtype=jnp.int32)
    flips = jnp.sum(deltas[:, :, None] * (orbitals[:, :, None] == columns[None, None, :]).astype(jnp.float32), axis=0)
    slot_pre = base_pre + jnp.dot(flips.astype(jnp.bfloat16), first_weight, preferred_element_type=jnp.float32)
    slot_hidden = jnp.tanh(slot_pre).astype(jnp.bfloat16)
    slot_mid = jnp.tanh(jnp.dot(slot_hidden, second_weight, preferred_element_type=jnp.float32))
    return jnp.dot(slot_mid, readout.T, precision=PRECISE)


def reference(occupations, connection_counts, connection_orbitals, connection_elements, laser_step, first_weight, first_bias, second_weight, readout):
    field = FIELD_SCALE * jnp.sin(FIELD_RATE * laser_step.astype(jnp.float32))
    pre = jnp.dot(occupations.astype(jnp.bfloat16), first_weight, preferred_element_type=jnp.float32) + first_bias
    hidden = jnp.tanh(pre).astype(jnp.bfloat16)
    mid = jnp.tanh(jnp.dot(hidden, second_weight, preferred_element_type=jnp.float32))
    logs = jnp.dot(mid, readout.T, precision=PRECISE)
    blocks = SAMPLES // S_DEV
    cumulative = jnp.cumsum(connection_counts.reshape(blocks, S_DEV), axis=1, dtype=jnp.int32)
    orbital_blocks = connection_orbitals.reshape(UPD, blocks * N_PARAMS, CAP).transpose(1, 0, 2)
    element_blocks = connection_elements.reshape(2, blocks * N_PARAMS, CAP).transpose(1, 0, 2)

    def one_device(index):
        block = index // N_PARAMS
        place = index % N_PARAMS
        positions = (place + N_PARAMS * jnp.arange(CAP, dtype=jnp.int32)).astype(jnp.int32)
        ends = cumulative[block]
        parent = jnp.sum((ends[None, :] <= positions[:, None]).astype(jnp.int32), axis=1, dtype=jnp.int32)
        parent = jnp.minimum(parent, S_DEV - 1)
        used = positions < ends[-1]
        global_parent = (block * S_DEV + parent).astype(jnp.int32)
        orbitals = orbital_blocks[index]
        elements = element_blocks[index]
        picked = jnp.take_along_axis(jnp.take(occupations, global_parent, axis=0), orbitals.T, axis=1).T
        deltas = 1.0 - 2.0 * picked.astype(jnp.float32)
        slot_logs = slot_values(jnp.take(pre, global_parent, axis=0), orbitals, deltas, first_weight, second_weight, readout)
        diff = slot_logs - jnp.take(logs, global_parent, axis=0)
        magnitude = jnp.exp(diff[:, 0])
        ratio = jnp.stack([magnitude * jnp.cos(diff[:, 1]), magnitude * jnp.sin(diff[:, 1])])
        weight = elements[0] + field * elements[1]
        contrib = jnp.where(used[None, :], weight[None, :] * ratio, 0.0)
        target = jnp.where(used, global_parent, SAMPLES).astype(jnp.int32)
        return contrib, target

    contribs, targets = lax.map(one_device, jnp.arange(blocks * N_PARAMS, dtype=jnp.int32))
    summed = jax.ops.segment_sum(contribs.transpose(0, 2, 1).reshape(-1, 2), targets.reshape(-1), num_segments=SAMPLES + 1)
    local_energy = summed[:SAMPLES].T

    hidden_full = hidden.astype(jnp.float32)
    slope = 1.0 - mid * mid
    slope_re = slope * readout[0]
    slope_im = slope * readout[1]
    total = float(SAMPLES)
    obar_re = jnp.dot(hidden_full.T, slope_re, precision=PRECISE) / total
    obar_im = jnp.dot(hidden_full.T, slope_im, precision=PRECISE) / total
    emean = jnp.sum(local_energy, axis=1) / total
    centered = local_energy - emean[:, None]
    force = jnp.dot(hidden_full.T, slope_re * centered[1][:, None] - slope_im * centered[0][:, None], precision=PRECISE) / total

    def project(vector):
        lifted = jnp.dot(hidden_full, vector, precision=PRECISE)
        raw = jnp.stack([jnp.sum(lifted * slope_re, axis=1), jnp.sum(lifted * slope_im, axis=1)])
        means = jnp.stack([jnp.sum(obar_re * vector), jnp.sum(obar_im * vector)])
        return raw - means[:, None]

    def metric(vector):
        coeffs = project(vector)
        back = slope_re * coeffs[0][:, None] + slope_im * coeffs[1][:, None]
        return jnp.dot(hidden_full.T, back, precision=PRECISE) / total + DIAG_SHIFT * vector

    solution = jnp.zeros_like(force)
    residual = force
    direction = force
    norm_now = jnp.sum(residual * residual)
    for turn in range(ITERS):
        image = metric(direction)
        alpha = norm_now / jnp.sum(direction * image)
        solution = solution + alpha * direction
        residual = residual - alpha * image
        norm_next = jnp.sum(residual * residual)
        direction = residual + (norm_next / norm_now) * direction
        norm_now = norm_next
    change = project(solution)
    return local_energy, change
```

```python
import functools

import jax
import jax.numpy as jnp
from jax import lax
from jax.experimental import pallas as pl
from jax.experimental.pallas import tpu as pltpu
from jax.sharding import PartitionSpec as P

FIELD_SCALE = 0.8
FIELD_RATE = 0.0123
DIAG_SHIFT = 0.01
MESH = pl.DeviceIdType.MESH
F32 = jnp.float32
BF16 = jnp.bfloat16


def sincos(x):
    n = jnp.floor(x * 0.6366197723675814 + 0.5)
    r = x - n * 1.5703125
    r = r - n * 4.8351287841796875e-4
    r = r - n * 3.1385570764541626e-7
    r = r - n * 6.0771005065061922e-11
    z = r * r
    s = r + r * z * (-1.6666654611e-1 + z * (8.3321608736e-3 - z * 1.9515295891e-4))
    c = 1.0 - 0.5 * z + z * z * (
        4.166664568298827e-2 + z * (-1.388731625493765e-3 + z * 2.443315711809948e-5)
    )
    quad = n - 4.0 * jnp.floor(n * 0.25)
    odd = (quad == 1.0) | (quad == 3.0)
    sin = jnp.where(odd, c, s)
    cos = jnp.where(odd, s, c)
    sin = jnp.where(quad >= 2.0, -sin, sin)
    cos = jnp.where((quad == 1.0) | (quad == 2.0), -cos, cos)
    return sin, cos


def parts3(x):
    hi = x.astype(BF16).astype(F32)
    rest = x - hi
    mid = rest.astype(BF16).astype(F32)
    return hi, mid, rest - mid


def pack_rows(rows, height):
    width = rows[0].shape[1]
    place = lax.broadcasted_iota(jnp.int32, (height, width), 0)
    out = jnp.zeros((height, width), F32)
    for i, row in enumerate(rows):
        out = jnp.where(place == i, jnp.broadcast_to(row, (height, width)), out)
    return out


def nn(a, b):
    return lax.dot_general(a, b, (((1,), (0,)), ((), ())), preferred_element_type=F32)


def nt(a, b):
    return lax.dot_general(a, b, (((1,), (1,)), ((), ())), preferred_element_type=F32)


def tn(a, b):
    return lax.dot_general(a, b, (((0,), (0,)), ((), ())), preferred_element_type=F32)


def kernel(
    n_params,
    n_groups,
    occ_ref,
    counts_ref,
    orb_ref,
    elem_ref,
    step_ref,
    w1_ref,
    bias_ref,
    w2_ref,
    readout_ref,
    out_ref,
    occ_mine,
    occ_col,
    occ_row,
    w2_full,
    slot_hid,
    pick,
    kt_hi,
    kt_lo,
    e_msg,
    e_buf,
    y_msg,
    y_buf,
    z_msg,
    z_buf,
    s_msg,
    s_buf,
    change_buf,
    w2_send,
    w2_recv,
    col_send,
    col_recv,
    row_send,
    row_recv,
    e_send,
    e_recv,
    y_send,
    y_recv,
    z_send,
    z_recv,
    s_send,
    s_recv,
):
    samples, orbitals = occ_ref.shape
    slots = orb_ref.shape[1]
    depth = w2_ref.shape[0]
    hid2 = w2_ref.shape[1]
    pn = n_params
    cn = n_groups
    g = cn // pn
    block = g * samples
    total = float(block * cn)

    b = lax.axis_index("samples")
    p = lax.axis_index("params")
    k = b // g
    q = b % g
    l = q * pn + p
    alone = l == k

    def member(group, m):
        return (group * g + m // pn, m % pn)

    barrier = pltpu.get_barrier_semaphore()

    def signal(device):
        pl.semaphore_signal(barrier, inc=1, device_id=device, device_id_type=MESH)

    def greet(d, carry):
        signal(member(k, lax.rem(l + d, cn)))
        j = lax.rem(k + d, cn)
        signal((j * g + k // pn, k % pn))
        return carry

    lax.fori_loop(1, cn, greet, 0)

    @pl.when(jnp.logical_not(alone))
    def _():
        signal((k * g + k // pn, k % pn))

    for i in range(g):

        @pl.when(jnp.logical_not(alone & (q == i)))
        def _():
            signal((l * g + i, k % pn))

    occ = occ_ref[...].astype(F32)
    occ_mine[...] = jnp.zeros_like(occ_mine)
    occ_mine[:, :orbitals] = occ.astype(BF16)

    pl.semaphore_wait(barrier, jnp.where(alone, 2 * cn + g - 3, 2 * cn + g - 1))

    half = depth // 2
    copies = []

    def start(src, dst, send, recv, device):
        copy = pltpu.make_async_remote_copy(
            src_ref=src, dst_ref=dst, send_sem=send, recv_sem=recv, device_id=device, device_id_type=MESH
        )
        copy.start()
        return copy

    p_core = p + 1 - 2 * (p % 2)
    b_pair = b + 1 - 2 * (b % 2)
    whole = pl.ds(pl.multiple_of(p * depth, depth), depth)
    copies.append(start(w2_ref, w2_full.at[whole], w2_send.at[0], w2_recv.at[0], (b, p_core)))
    if pn == 4:
        for d in (0, 1):
            far = (p // 2) * (-2) + 2 + (p % 2 + d) % 2
            for h, to in ((0, b), (1, b_pair)):
                rows = pl.ds(pl.multiple_of(p * depth + h * half, half), half)
                i = 1 + d * 2 + h
                copies.append(
                    start(w2_ref.at[pl.ds(h * half, half)], w2_full.at[rows], w2_send.at[i], w2_recv.at[i], (to, far))
                )
    for d in range(1, g):
        i = lax.rem(q + d, g)
        copies.append(start(occ_mine, occ_col.at[q], col_send.at[d], col_recv.at[g - d], (k * g + i, p)))

    def row_copy(t):
        kk = p + pn * t
        return pltpu.make_async_remote_copy(
            src_ref=occ_mine,
            dst_ref=occ_row.at[q],
            send_sem=row_send.at[t],
            recv_sem=row_recv.at[q],
            device_id=(kk * g + k // pn, k % pn),
            device_id_type=MESH,
        )

    for t in range(cn // pn):

        @pl.when(jnp.logical_not(alone & (k == p + pn * t)))
        def _():
            row_copy(t).start()

    w2_full[whole] = w2_ref[...]
    occ_col[q] = occ_mine[...]

    @pl.when(alone)
    def _():
        occ_row[q] = occ_mine[...]

    counts = jnp.broadcast_to(counts_ref[...].astype(F32), (8, samples))
    r_id = lax.broadcasted_iota(jnp.int32, (samples, samples), 0)
    c_id = lax.broadcasted_iota(jnp.int32, (samples, samples), 1)
    upto = (r_id <= c_id).astype(BF16)
    c_hi, c_mid, c_lo = parts3(counts)
    ends = nn(c_hi.astype(BF16), upto) + nn(c_mid.astype(BF16), upto) + nn(c_lo.astype(BF16), upto)
    begins = ends - counts
    ends, begins = ends[0:1], begins[0:1]
    position = (p + pn * lax.broadcasted_iota(jnp.int32, (slots, samples), 0)).astype(F32)
    pick[...] = ((begins <= position) & (position < ends)).astype(BF16)
    occ_t = occ.T.astype(BF16)
    w1 = w1_ref[...]
    bias = bias_ref[...]
    chunk = 256
    for start_row in range(0, slots, chunk):
        rows = slice(start_row, start_row + chunk)
        base = nt(occ_t, pick[rows])
        column = lax.broadcasted_iota(jnp.int32, (orbitals, chunk), 0)
        orb = orb_ref[:, rows]
        flip = orb[0:1] == column
        for u in range(1, orb_ref.shape[0]):
            flip = flip | (orb[u : u + 1] == column)
        flipped = jnp.where(flip, 1.0 - base, base).astype(BF16)
        slot_hid[rows] = jnp.tanh(tn(flipped, w1) + bias).astype(BF16)
    hidden = jnp.tanh(nn(occ_mine[:, :orbitals], w1) + bias).astype(BF16)

    for copy in copies[: 5 if pn == 4 else 1]:
        copy.wait_recv()
    w2 = w2_full[...]

    readout = readout_ref[...]
    r_rows = pack_rows([x[i : i + 1] for x in parts3(readout) for i in range(2)], 16).astype(BF16)

    def logs_of(hid):
        mid = jnp.tanh(nn(hid, w2))
        hi = mid.astype(BF16)
        lo = (mid - hi.astype(F32)).astype(BF16)
        out = nt(r_rows, hi) + nt(r_rows, lo)
        return out[0:2] + out[2:4] + out[4:6]

    logs = logs_of(hidden)
    slot_logs = logs_of(slot_hid[...])
    l_rows = pack_rows([x[i : i + 1] for x in parts3(logs) for i in range(2)], 16).astype(BF16)
    parent_logs = nt(l_rows, pick[...])
    parent_logs = parent_logs[0:2] + parent_logs[2:4] + parent_logs[4:6]
    diff = slot_logs - parent_logs
    angle = jnp.full((1, slots), step_ref[0, 0], jnp.int32).astype(F32) * FIELD_RATE
    field = FIELD_SCALE * sincos(angle)[0]
    elem = elem_ref[...]
    weight = elem[0:1] + field * elem[1:2]
    slot_at = (p + pn * lax.broadcasted_iota(jnp.int32, (1, slots), 1)).astype(F32)
    used = slot_at < ends[0:1, samples - 1 : samples]
    size = jnp.exp(diff[0:1])
    sin, cos = sincos(diff[1:2])
    contrib = [jnp.where(used, weight * (size * cos), 0.0), jnp.where(used, weight * (size * sin), 0.0)]
    splits = [parts3(x) for x in contrib]
    e_rows = pack_rows([splits[i][j] for j in range(3) for i in range(2)], 16).astype(BF16)
    energy = nn(e_rows, pick[...])
    energy = energy[0:2] + energy[2:4] + energy[4:6]
    e_msg[...] = jnp.zeros_like(e_msg)
    e_msg[0:2, :samples] = energy

    def e_copy(d):
        return pltpu.make_async_remote_copy(
            src_ref=e_msg,
            dst_ref=e_buf.at[l],
            send_sem=e_send.at[d],
            recv_sem=e_recv.at[l],
            device_id=member(k, lax.rem(l + d, cn)),
            device_id_type=MESH,
        )

    def send_e(d, carry):
        e_copy(d).start()
        return carry

    lax.fori_loop(1, cn, send_e, 0)
    e_buf[l] = e_msg[...]

    for d in range(1, g):
        pltpu.make_async_remote_copy(
            src_ref=occ_mine,
            dst_ref=occ_col.at[lax.rem(q + d, g)],
            send_sem=col_send.at[d],
            recv_sem=col_recv.at[d],
            device_id=(b, p_core),
            device_id_type=MESH,
        ).wait_recv()
    for i in range(g):

        @pl.when(jnp.logical_not(alone & (q == i)))
        def _():
            pltpu.make_async_remote_copy(
                src_ref=occ_mine,
                dst_ref=occ_row.at[i],
                send_sem=row_send.at[0],
                recv_sem=row_recv.at[i],
                device_id=(b, p_core),
                device_id_type=MESH,
            ).wait_recv()

    def hidden_of(ref):
        rows = ref[...].reshape(block, ref.shape[2])[:, :orbitals]
        return jnp.tanh(nn(rows, w1) + bias).astype(BF16)

    def slope_of(hid):
        mid = jnp.tanh(nn(hid, w2))
        return 1.0 - mid * mid

    hid_k = hidden_of(occ_col)
    hid_l = hidden_of(occ_row)
    slope_k = slope_of(hid_k)
    slope_l = slope_of(hid_l)
    gram = nt(hid_k, hid_l)
    l_hi = slope_l.astype(BF16)
    l_lo = (slope_l - l_hi.astype(F32)).astype(BF16)
    ones = []
    pairs = (readout[0:1] * readout[0:1], readout[0:1] * readout[1:2], readout[1:2] * readout[1:2])
    for t, pair in enumerate(pairs):
        scaled = slope_k * pair
        s_hi = scaled.astype(BF16)
        s_lo = (scaled - s_hi.astype(F32)).astype(BF16)
        kt = gram * (nt(s_hi, l_hi) + (nt(s_lo, l_hi) + nt(s_hi, l_lo)))
        hi = kt.astype(BF16)
        kt_hi[t] = hi
        kt_lo[t] = (kt - hi.astype(F32)).astype(BF16)
        ones.append(jnp.sum(kt, axis=0, keepdims=True))

    def apply(va, vb):
        ma = jnp.sum(va, axis=1, keepdims=True) * (1.0 / block)
        mb = jnp.sum(vb, axis=1, keepdims=True) * (1.0 / block)
        rows = pack_rows([*parts3(va - ma), *parts3(vb - mb)], 16).astype(BF16)
        outs = []
        for t in range(3):
            out = nn(rows, kt_hi[t]) + nn(rows, kt_lo[t])
            outs.append((out[0:1] + out[1:2] + out[2:3], out[3:4] + out[4:5] + out[5:6]))
        y_re = outs[0][0] + outs[1][1] + (ones[0] * ma + ones[1] * mb)
        y_im = outs[1][0] + outs[2][1] + (ones[1] * ma + ones[2] * mb)
        return y_re, y_im

    def across(msg, buf, send, recv):
        def copy(d):
            return pltpu.make_async_remote_copy(
                src_ref=msg,
                dst_ref=buf.at[k],
                send_sem=send.at[d],
                recv_sem=recv.at[k],
                device_id=member(l, lax.rem(l + d, cn)),
                device_id_type=MESH,
            )

        def begin(d, carry):
            copy(d).start()
            return carry

        lax.fori_loop(1, cn, begin, 0)

        @pl.when(jnp.logical_not(alone))
        def _():
            copy(0).start()

        @pl.when(alone)
        def _():
            buf[k] = msg[...]

        def arrived(j):
            pltpu.make_async_remote_copy(
                src_ref=msg,
                dst_ref=buf.at[j],
                send_sem=send.at[0],
                recv_sem=recv.at[j],
                device_id=(b, p_core),
                device_id_type=MESH,
            ).wait_recv()

        def finish(d, carry):
            arrived(lax.rem(k + d, cn))
            return carry

        lax.fori_loop(1, cn, finish, 0)

        @pl.when(jnp.logical_not(alone))
        def _():
            arrived(k)

    def drain(msg, buf, send):
        def one(d):
            pltpu.make_async_remote_copy(
                src_ref=msg,
                dst_ref=buf.at[k],
                send_sem=send.at[d],
                recv_sem=send.at[d],
                device_id=(b, p_core),
                device_id_type=MESH,
            ).wait_send()

        def step(d, carry):
            one(d)
            return carry

        lax.fori_loop(1, cn, step, 0)

        @pl.when(jnp.logical_not(alone))
        def _():
            one(0)

    def e_wait(d, carry):
        pltpu.make_async_remote_copy(
            src_ref=e_msg,
            dst_ref=e_buf.at[lax.rem(l + d, cn)],
            send_sem=e_send.at[0],
            recv_sem=e_recv.at[lax.rem(l + d, cn)],
            device_id=(b, p_core),
            device_id_type=MESH,
        ).wait_recv()
        return carry

    lax.fori_loop(1, cn, e_wait, 0)
    sums = []
    for i in range(g):
        acc = e_buf[i * pn]
        for j in range(1, pn):
            acc = acc + e_buf[i * pn + j]
        sums.append(acc)
    tiles = [sums[i] + pltpu.roll(sums[i + 1], samples, 1) for i in range(0, g, 2)]
    energies = jnp.concatenate(tiles, axis=1)
    mine = e_buf[q * pn]
    for j in range(1, pn):
        mine = mine + e_buf[q * pn + j]
    out_ref[0:2] = mine[0:2]

    ea = energies[1:2] * (1.0 / total)
    eb = energies[0:1] * (-1.0 / total)
    y_re, y_im = apply(ea, eb)
    ma = jnp.broadcast_to(jnp.sum(ea, axis=1, keepdims=True) * (1.0 / total), ea.shape)
    mb = jnp.broadcast_to(jnp.sum(eb, axis=1, keepdims=True) * (1.0 / total), eb.shape)
    y_msg[...] = pack_rows([y_re, y_im, *ones, ma, mb], 8)
    across(y_msg, y_buf, y_send, y_recv)
    y = y_buf[0]
    for j in range(1, cn):
        y = y + y_buf[j]
    one_rr, one_ri, one_ii = y[2:3], y[3:4], y[4:5]
    ga, gb = y[5:6], y[6:7]
    fa, fb = ea - ga, eb - gb
    f_re = y[0:1] - (one_rr * ga + one_ri * gb)
    f_im = y[1:2] - (one_ri * ga + one_ii * gb)

    ha = f_re * (1.0 / total) + DIAG_SHIFT * fa
    hb = f_im * (1.0 / total) + DIAG_SHIFT * fb
    z_re, z_im = apply(ha, hb)
    ma = jnp.broadcast_to(jnp.sum(f_re, axis=1, keepdims=True) * (1.0 / total), ea.shape)
    mb = jnp.broadcast_to(jnp.sum(f_im, axis=1, keepdims=True) * (1.0 / total), eb.shape)
    z_msg[...] = pack_rows([z_re, z_im, ma, mb], 8)
    across(z_msg, z_buf, z_send, z_recv)
    z = z_buf[0]
    for j in range(1, cn):
        z = z + z_buf[j]
    f_mean_re, f_mean_im = z[2:3], z[3:4]
    ga, gb = f_mean_re * (1.0 / total), f_mean_im * (1.0 / total)
    a_re = z[0:1] - (one_rr * ga + one_ri * gb)
    a_im = z[1:2] - (one_ri * ga + one_ii * gb)
    ha, hb = ha - ga, hb - gb

    def inner(ua, ub, va, vb):
        return jnp.sum(ua * va + ub * vb, axis=1, keepdims=True)

    mean_re = jnp.sum(a_re, axis=1, keepdims=True) * (1.0 / block)
    mean_im = jnp.sum(a_im, axis=1, keepdims=True) * (1.0 / block)
    da, db = a_re - mean_re, a_im - mean_im
    scalars = [
        inner(fa, fb, f_re, f_im),
        inner(fa, fb, a_re, a_im),
        inner(ha, hb, a_re, a_im),
        inner(da, db, da, db),
        mean_re,
        mean_im,
    ]
    s_msg[...] = pack_rows([jnp.broadcast_to(x, (1, 128)) for x in scalars], 8)
    across(s_msg, s_buf, s_send, s_recv)
    s = s_buf[0]
    for j in range(1, cn):
        s = s + s_buf[j]
    means = s * (1.0 / cn)
    spread = jnp.square(s_buf[0] - means)
    for j in range(1, cn):
        spread = spread + jnp.square(s_buf[j] - means)
    ff, f_af, af_af = s[0:1, 0:1], s[1:2, 0:1], s[2:3, 0:1]
    centered = s[3:4, 0:1] + float(block) * (spread[4:5, 0:1] + spread[5:6, 0:1])
    af_aaf = centered * (1.0 / total) + DIAG_SHIFT * af_af
    alpha0 = ff / f_af
    rr = ff - 2.0 * alpha0 * f_af + alpha0 * alpha0 * af_af
    beta = rr / ff
    near = 1.0 + beta
    curv = near * near * f_af - 2.0 * near * alpha0 * af_af + alpha0 * alpha0 * af_aaf
    alpha1 = rr / curv
    on_f = alpha0 + alpha1 * near
    on_af = alpha1 * alpha0
    pf_re, pf_im = f_re - f_mean_re, f_im - f_mean_im
    pa_re, pa_im = a_re - means[4:5, 0:1], a_im - means[5:6, 0:1]
    change = pack_rows([on_f * pf_re - on_af * pa_re, on_f * pf_im - on_af * pa_im], 8)
    for i in range(block // 128):
        change_buf[i] = change[:, i * 128 : (i + 1) * 128]
    tile = change_buf[(q * samples) // 128]
    odd = jnp.full(tile.shape, q % 2, jnp.int32) == 1
    tile = jnp.where(odd, pltpu.roll(tile, samples, 1), tile)
    out_ref[2:4] = tile[0:2]

    for copy in copies:
        copy.wait_send()
    for t in range(cn // pn):

        @pl.when(jnp.logical_not(alone & (k == p + pn * t)))
        def _():
            row_copy(t).wait_send()

    def e_drain(d, carry):
        e_copy(d).wait_send()
        return carry

    lax.fori_loop(1, cn, e_drain, 0)
    drain(y_msg, y_buf, y_send)
    drain(z_msg, z_buf, z_send)
    drain(s_msg, s_buf, s_send)


def body(n_params, n_samples, occ, counts, orb, elem, step, w1, bias, w2, readout):
    devices = n_params * n_samples
    cn = 1
    while cn * cn < devices:
        cn *= 2
    g = cn // n_params
    samples = occ.shape[0]
    slots = orb.shape[1]
    depth, hid2 = w2.shape
    hid = w1.shape[1]
    block = g * samples
    vmem = pl.BlockSpec(memory_space=pltpu.VMEM)
    dma = pltpu.SemaphoreType.DMA
    out = pl.pallas_call(
        functools.partial(kernel, n_params, cn),
        out_shape=jax.ShapeDtypeStruct((4, 128), F32),
        in_specs=[vmem, vmem, vmem, vmem, pl.BlockSpec(memory_space=pltpu.SMEM), vmem, vmem, vmem, vmem],
        out_specs=vmem,
        scratch_shapes=[
            pltpu.VMEM((samples, 256), BF16),
            pltpu.VMEM((g, samples, 256), BF16),
            pltpu.VMEM((g, samples, 256), BF16),
            pltpu.VMEM((depth * n_params, hid2), BF16),
            pltpu.VMEM((slots, hid), BF16),
            pltpu.VMEM((slots, samples), BF16),
            pltpu.VMEM((3, block, block), BF16),
            pltpu.VMEM((3, block, block), BF16),
            pltpu.VMEM((8, 128), F32),
            pltpu.VMEM((cn, 8, 128), F32),
            pltpu.VMEM((8, block), F32),
            pltpu.VMEM((cn, 8, block), F32),
            pltpu.VMEM((8, block), F32),
            pltpu.VMEM((cn, 8, block), F32),
            pltpu.VMEM((8, 128), F32),
            pltpu.VMEM((cn, 8, 128), F32),
            pltpu.VMEM((block // 128, 8, 128), F32),
            dma((5,)),
            dma((5,)),
            dma((g,)),
            dma((g,)),
            dma((cn // n_params,)),
            dma((g,)),
            dma((cn,)),
            dma((cn,)),
            dma((cn,)),
            dma((cn,)),
            dma((cn,)),
            dma((cn,)),
            dma((cn,)),
            dma((cn,)),
        ],
        compiler_params=pltpu.CompilerParams(
            collective_id=0, has_side_effects=True, vmem_limit_bytes=40 * 1024 * 1024
        ),
    )(
        occ,
        counts.reshape(1, samples),
        orb,
        elem,
        step.reshape(1, 1),
        w1,
        bias.reshape(1, hid),
        w2,
        readout,
    )
    return out[0:2, :samples], out[2:4, :samples]


def solution(mesh):
    return jax.shard_map(
        functools.partial(body, mesh.shape["params"], mesh.shape["samples"]),
        mesh=mesh,
        in_specs=(
            P("samples", None),
            P("samples"),
            P(None, ("samples", "params")),
            P(None, ("samples", "params")),
            P(),
            P(),
            P(),
            P("params", None),
            P(),
        ),
        out_specs=(P(None, "samples"), P(None, "samples")),
        check_vma=False,
    )
```

```python
import jax
import jax.numpy as jnp
from jax import lax
from jax.experimental import pallas as pl
from jax.experimental.pallas import tpu as pltpu
from jax.sharding import PartitionSpec as P

FIELD_SCALE = 0.8
FIELD_RATE = 0.0123
DIAG_SHIFT = 0.01
LINE = 8
PLANE = 8
PARAMS = 4
MESH = pl.DeviceIdType.MESH
F32 = jnp.float32
BF16 = jnp.bfloat16


def sincos(x):
    n = jnp.floor(x * 0.6366197723675814 + 0.5)
    r = x - n * 1.5703125
    r = r - n * 4.8351287841796875e-4
    r = r - n * 3.1385570764541626e-7
    r = r - n * 6.0771005065061922e-11
    z = r * r
    s = r + r * z * (-1.6666654611e-1 + z * (8.3321608736e-3 - z * 1.9515295891e-4))
    c = 1.0 - 0.5 * z + z * z * (
        4.166664568298827e-2 + z * (-1.388731625493765e-3 + z * 2.443315711809948e-5)
    )
    quad = n - 4.0 * jnp.floor(n * 0.25)
    odd = (quad == 1.0) | (quad == 3.0)
    sin = jnp.where(odd, c, s)
    cos = jnp.where(odd, s, c)
    sin = jnp.where(quad >= 2.0, -sin, sin)
    cos = jnp.where((quad == 1.0) | (quad == 2.0), -cos, cos)
    return sin, cos


def parts3(x):
    hi = x.astype(BF16).astype(F32)
    rest = x - hi
    mid = rest.astype(BF16).astype(F32)
    return hi, mid, rest - mid


def pack_rows(rows, height):
    width = rows[0].shape[1]
    place = lax.broadcasted_iota(jnp.int32, (height, width), 0)
    out = jnp.zeros((height, width), F32)
    for i, row in enumerate(rows):
        out = jnp.where(place == i, jnp.broadcast_to(row, (height, width)), out)
    return out


def nn(a, b):
    return lax.dot_general(a, b, (((1,), (0,)), ((), ())), preferred_element_type=F32)


def nt(a, b):
    return lax.dot_general(a, b, (((1,), (1,)), ((), ())), preferred_element_type=F32)


def tn(a, b):
    return lax.dot_general(a, b, (((0,), (0,)), ((), ())), preferred_element_type=F32)


def kernel(
    occ_hbm,
    counts_hbm,
    orb_hbm,
    elem_hbm,
    step_hbm,
    w1_hbm,
    bias_hbm,
    w2_hbm,
    readout_hbm,
    out_ref,
    occ_ref,
    counts_ref,
    orb_ref,
    elem_ref,
    step_ref,
    w1_ref,
    bias_ref,
    w2_ref,
    readout_ref,
    in_sem,
    occ_mine,
    occ_line,
    occ_plane,
    w2_full,
    slot_hid,
    pick,
    kt_hi,
    kt_lo,
    e_msg,
    e_buf,
    kp_msg,
    kp_buf,
    kl_msg,
    kl_buf,
    y_msg,
    y_buf,
    z_msg,
    z_buf,
    s_msg,
    s_buf,
    own_buf,
    w2_send,
    w2_recv,
    op_send,
    op_recv,
    ol_send,
    ol_recv,
    e_send,
    e_recv,
    kp_send,
    kp_recv,
    kl_send,
    kl_recv,
    y_send,
    y_recv,
    z_send,
    z_recv,
    s_send,
    s_recv,
):
    outside = (occ_hbm, w2_hbm, w1_hbm, orb_hbm, counts_hbm, bias_hbm, elem_hbm, step_hbm, readout_hbm)
    inside = (occ_ref, w2_ref, w1_ref, orb_ref, counts_ref, bias_ref, elem_ref, step_ref, readout_ref)
    loads = [pltpu.make_async_copy(a, c, in_sem.at[i]) for i, (a, c) in enumerate(zip(outside, inside))]
    for load in loads:
        load.start()
    samples, orbitals = occ_ref.shape
    slots = orb_ref.shape[1]
    depth = w2_ref.shape[0]
    pn = PARAMS
    block = LINE * samples
    total = float(block * PLANE)

    b = lax.axis_index("samples")
    p = lax.axis_index("params")
    z = b // PLANE
    w = b % PLANE
    p_core = p + 1 - 2 * (p % 2)
    p_far = p + 2 - 4 * (p // 2)
    p_cross = p_far + 1 - 2 * (p_far % 2)
    b_pair = b + 1 - 2 * (b % 2)

    def line_peer(d):
        to = lax.rem(z + d, LINE)
        return to, (to * PLANE + w, p)

    def plane_peer(d):
        y, half = w // 2, w % 2
        to_y = lax.rem(y + d // 2, PLANE // 2)
        if d % 2:
            to = to_y * 2 + 1 - half
            return to, (z * PLANE + to, p_far)
        to = to_y * 2 + half
        return to, (z * PLANE + to, p)

    LINE_ORDER = (4, 3, 5, 2, 6, 1, 7)
    PLANE_ORDER = (5, 4, 3, 7, 2, 6, 1)

    def energy_peer(d):
        return lax.rem(z + d // pn, LINE) * PLANE + w, lax.rem(p + lax.rem(d, pn), pn)

    def copy_to(src, dst, send, recv, device):
        return pltpu.make_async_remote_copy(
            src_ref=src, dst_ref=dst, send_sem=send, recv_sem=recv, device_id=device, device_id_type=MESH
        )

    def spread(peer, order, me, msg, buf, send, recv):
        for d in order:
            copy_to(msg, buf.at[me], send.at[d], recv.at[me], peer(d)[1]).start()
        buf[me] = msg[...]

    def collect(peer, order, msg, buf, send, recv):
        for d in order:
            place, device = peer(d)
            copy_to(msg, buf.at[place], send.at[d], recv.at[place], device).wait_recv()

    def drain(peer, order, me, msg, buf, send, recv):
        for d in order:
            copy_to(msg, buf.at[me], send.at[d], recv.at[me], peer(d)[1]).wait_send()

    line = (line_peer, LINE_ORDER)
    plane = (plane_peer, PLANE_ORDER)

    barrier = pltpu.get_barrier_semaphore()

    def signal(device):
        pl.semaphore_signal(barrier, inc=1, device_id=device, device_id_type=MESH)

    signal((b_pair, p_cross))
    for d in PLANE_ORDER:
        signal(plane_peer(d)[1])

    def greet(d, carry):
        signal(energy_peer(d))
        return carry

    lax.fori_loop(1, LINE * pn, greet, 0)

    loads[0].wait()
    occ = occ_ref[...].astype(F32)
    occ_mine[...] = jnp.zeros_like(occ_mine)
    occ_mine[:, :orbitals] = occ.astype(BF16)
    loads[1].wait()

    pl.semaphore_wait(barrier, LINE * pn - 1 + PLANE - 1 + 1)

    half = depth // 2
    whole = pl.ds(pl.multiple_of(p * depth, depth), depth)
    w2_copies = []
    for d, far in ((0, p_far), (1, p_cross)):
        for h, to in ((0, b), (1, b_pair)):
            rows = pl.ds(pl.multiple_of(p * depth + h * half, half), half)
            i = 1 + d * 2 + h
            w2_copies.append(
                copy_to(w2_ref.at[pl.ds(h * half, half)], w2_full.at[rows], w2_send.at[i], w2_recv.at[i], (to, far))
            )
    w2_copies.append(copy_to(w2_ref, w2_full.at[whole], w2_send.at[0], w2_recv.at[0], (b, p_core)))
    for copy in w2_copies:
        copy.start()
    spread(*plane, w, occ_mine, occ_plane, op_send, op_recv)
    spread(*line, z, occ_mine, occ_line, ol_send, ol_recv)
    w2_full[whole] = w2_ref[...]

    for load in loads[2:]:
        load.wait()
    counts = jnp.broadcast_to(counts_ref[...].astype(F32), (8, samples))
    r_id = lax.broadcasted_iota(jnp.int32, (samples, samples), 0)
    c_id = lax.broadcasted_iota(jnp.int32, (samples, samples), 1)
    upto = (r_id <= c_id).astype(BF16)
    c_hi, c_mid, c_lo = parts3(counts)
    ends = nn(c_hi.astype(BF16), upto) + nn(c_mid.astype(BF16), upto) + nn(c_lo.astype(BF16), upto)
    begins = ends - counts
    ends, begins = ends[0:1], begins[0:1]
    position = (p + pn * lax.broadcasted_iota(jnp.int32, (slots, samples), 0)).astype(F32)
    pick[...] = ((begins <= position) & (position < ends)).astype(BF16)
    occ_t = occ.T.astype(BF16)
    w1 = w1_ref[...]
    bias = bias_ref[...]
    chunk = 256
    for start_row in range(0, slots, chunk):
        rows = slice(start_row, start_row + chunk)
        base = nt(occ_t, pick[rows])
        column = lax.broadcasted_iota(jnp.int32, (orbitals, chunk), 0)
        orb = orb_ref[:, rows]
        flip = orb[0:1] == column
        for u in range(1, orb_ref.shape[0]):
            flip = flip | (orb[u : u + 1] == column)
        flipped = jnp.where(flip, 1.0 - base, base).astype(BF16)
        slot_hid[rows] = jnp.tanh(tn(flipped, w1) + bias).astype(BF16)
    hidden = jnp.tanh(nn(occ_mine[:, :orbitals], w1) + bias).astype(BF16)

    for copy in w2_copies:
        copy.wait_recv()
    w2 = w2_full[...]

    readout = readout_ref[...]
    r_rows = pack_rows([x[i : i + 1] for x in parts3(readout) for i in range(2)], 16).astype(BF16)

    def logs_of(hid):
        mid = jnp.tanh(nn(hid, w2))
        hi = mid.astype(BF16)
        lo = (mid - hi.astype(F32)).astype(BF16)
        out = nt(r_rows, hi) + nt(r_rows, lo)
        return out[0:2] + out[2:4] + out[4:6]

    logs = logs_of(hidden)
    slot_logs = logs_of(slot_hid[...])
    l_rows = pack_rows([x[i : i + 1] for x in parts3(logs) for i in range(2)], 16).astype(BF16)
    parent_logs = nt(l_rows, pick[...])
    parent_logs = parent_logs[0:2] + parent_logs[2:4] + parent_logs[4:6]
    diff = slot_logs - parent_logs
    angle = jnp.broadcast_to(step_ref[...].astype(F32), (1, slots)) * FIELD_RATE
    field = FIELD_SCALE * sincos(angle)[0]
    elem = elem_ref[...]
    weight = elem[0:1] + field * elem[1:2]
    slot_at = (p + pn * lax.broadcasted_iota(jnp.int32, (1, slots), 1)).astype(F32)
    used = slot_at < ends[0:1, samples - 1 : samples]
    size = jnp.exp(diff[0:1])
    sin, cos = sincos(diff[1:2])
    contrib = [jnp.where(used, weight * (size * cos), 0.0), jnp.where(used, weight * (size * sin), 0.0)]
    splits = [parts3(x) for x in contrib]
    e_rows = pack_rows([splits[i][j] for j in range(3) for i in range(2)], 16).astype(BF16)
    energy = nn(e_rows, pick[...])
    energy = energy[0:2] + energy[2:4] + energy[4:6]
    e_msg[...] = jnp.zeros_like(e_msg)
    e_msg[0:2, :samples] = energy

    me = z * pn + p

    def e_copy(d):
        return copy_to(e_msg, e_buf.at[me], e_send.at[d], e_recv.at[me], energy_peer(d))

    def send_e(d, carry):
        e_copy(d).start()
        return carry

    lax.fori_loop(1, LINE * pn, send_e, 0)
    e_buf[me] = e_msg[...]

    collect(*plane, occ_mine, occ_plane, op_send, op_recv)
    collect(*line, occ_mine, occ_line, ol_send, ol_recv)

    def hidden_of(ref):
        rows = ref[...].reshape(block, ref.shape[2])[:, :orbitals]
        return jnp.tanh(nn(rows, w1) + bias).astype(BF16)

    def slope_of(hid):
        mid = jnp.tanh(nn(hid, w2))
        return 1.0 - mid * mid

    hid_c = hidden_of(occ_line)
    hid_r = hidden_of(occ_plane)
    slope_c = slope_of(hid_c)
    slope_r = slope_of(hid_r)
    gram = nt(hid_c, hid_r)
    r_hi = slope_r.astype(BF16)
    r_lo = (slope_r - r_hi.astype(F32)).astype(BF16)
    ones = jnp.ones((16, block), BF16)
    ones_r, ones_c = [], []
    pairs = (readout[0:1] * readout[0:1], readout[0:1] * readout[1:2], readout[1:2] * readout[1:2])
    for t, pair in enumerate(pairs):
        scaled = slope_c * pair
        s_hi = scaled.astype(BF16)
        s_lo = (scaled - s_hi.astype(F32)).astype(BF16)
        kt = gram * (nt(s_hi, r_hi) + (nt(s_lo, r_hi) + nt(s_hi, r_lo)))
        hi = kt.astype(BF16)
        lo = (kt - hi.astype(F32)).astype(BF16)
        kt_hi[t] = hi
        kt_lo[t] = lo
        ones_r.append(jnp.sum(kt, axis=0, keepdims=True))
        ones_c.append((nt(ones, hi) + nt(ones, lo))[0:1])
    kp_msg[...] = pack_rows(ones_r, 8)
    kl_msg[...] = pack_rows(ones_c, 8)
    spread(*plane, w, kp_msg, kp_buf, kp_send, kp_recv)
    spread(*line, z, kl_msg, kl_buf, kl_send, kl_recv)

    def apply(va, vb, ones, mul):
        ma = jnp.sum(va, axis=1, keepdims=True) * (1.0 / block)
        mb = jnp.sum(vb, axis=1, keepdims=True) * (1.0 / block)
        rows = pack_rows([*parts3(va - ma), *parts3(vb - mb)], 16).astype(BF16)
        outs = []
        for t in range(3):
            out = mul(rows, kt_hi[t]) + mul(rows, kt_lo[t])
            outs.append((out[0:1] + out[1:2] + out[2:3], out[3:4] + out[4:5] + out[5:6]))
        y_re = outs[0][0] + outs[1][1] + (ones[0] * ma + ones[1] * mb)
        y_im = outs[1][0] + outs[2][1] + (ones[1] * ma + ones[2] * mb)
        return y_re, y_im

    def total_of(buf):
        acc = buf[0]
        for j in range(1, buf.shape[0]):
            acc = acc + buf[j]
        return acc

    def pieces(tiles):
        pairs = [tiles[i] + pltpu.roll(tiles[i + 1], samples, 1) for i in range(0, len(tiles), 2)]
        return jnp.concatenate(pairs, axis=1)

    lane = lax.broadcasted_iota(jnp.int32, (8, 128), 1)

    def piece(value, place):
        for i in range(block // 128):
            own_buf[i] = value[:, i * 128 : (i + 1) * 128]
        tile = own_buf[place // 2]
        odd = jnp.full(tile.shape, place % 2, jnp.int32) == 1
        tile = jnp.where(odd, pltpu.roll(tile, samples, 1), tile)
        return jnp.where(lane < samples, tile, 0.0)

    def e_wait(d, carry):
        to_b, to_p = energy_peer(d)
        place = (to_b // PLANE) * pn + to_p
        copy_to(e_msg, e_buf.at[place], e_send.at[d], e_recv.at[place], (to_b, to_p)).wait_recv()
        return carry

    lax.fori_loop(1, LINE * pn, e_wait, 0)

    def over_params(i):
        acc = e_buf[i * pn]
        for j in range(1, pn):
            acc = acc + e_buf[i * pn + j]
        return acc

    energies = pieces([over_params(i) for i in range(LINE)])
    mine = over_params(z)
    out_ref[0:2] = mine[0:2]

    ea = energies[1:2] * (1.0 / total)
    eb = energies[0:1] * (-1.0 / total)
    y_re, y_im = apply(ea, eb, ones_r, nn)
    y_msg[0:8] = pack_rows([y_re, y_im], 8)
    y_msg[2:4, 0:128] = mine[0:2]
    means = [jnp.sum(v, axis=1, keepdims=True) * (1.0 / total) for v in (ea, eb)]
    y_msg[2:4, 128:256] = pack_rows([jnp.broadcast_to(v, (1, 128)) for v in means], 2)
    spread(*plane, w, y_msg, y_buf, y_send, y_recv)
    collect(*plane, kp_msg, kp_buf, kp_send, kp_recv)
    collect(*plane, y_msg, y_buf, y_send, y_recv)
    k1 = total_of(kp_buf)
    y = total_of(y_buf)
    ga, gb = y[2:3, 128:129], y[3:4, 128:129]
    around = pieces([y_buf[i, :, 0:128] for i in range(PLANE)])
    fa = around[3:4] * (1.0 / total) - ga
    fb = around[2:3] * (-1.0 / total) - gb
    f_re = y[0:1] - (k1[0:1] * ga + k1[1:2] * gb)
    f_im = y[1:2] - (k1[1:2] * ga + k1[2:3] * gb)

    ha = f_re * (1.0 / total) + DIAG_SHIFT * fa
    hb = f_im * (1.0 / total) + DIAG_SHIFT * fb
    z_re, z_im = apply(ha, hb, ones_c, nt)
    z_msg[0:8] = pack_rows([z_re, z_im], 8)
    f_mine = piece(pack_rows([f_re, f_im], 8), w)
    z_msg[2:4, 0:128] = f_mine[0:2]
    norm = jnp.sum(fa * f_re + fb * f_im, axis=1, keepdims=True)
    means = [jnp.sum(v, axis=1, keepdims=True) * (1.0 / total) for v in (f_re, f_im)]
    z_msg[2:5, 128:256] = pack_rows([jnp.broadcast_to(v, (1, 128)) for v in (*means, norm)], 3)
    spread(*line, z, z_msg, z_buf, z_send, z_recv)
    ca, cb = ea - ga, eb - gb
    collect(*line, kl_msg, kl_buf, kl_send, kl_recv)
    collect(*line, z_msg, z_buf, z_send, z_recv)
    k1 = total_of(kl_buf)
    acc = total_of(z_buf)
    f_mean_re, f_mean_im, ff = acc[2:3, 128:129], acc[3:4, 128:129], acc[4:5, 128:129]
    ga, gb = f_mean_re * (1.0 / total), f_mean_im * (1.0 / total)
    a_re = acc[0:1] - (k1[0:1] * ga + k1[1:2] * gb)
    a_im = acc[1:2] - (k1[1:2] * ga + k1[2:3] * gb)
    along = pieces([z_buf[i, :, 0:128] for i in range(LINE)])
    ha = along[2:3] * (1.0 / total) - ga + DIAG_SHIFT * ca
    hb = along[3:4] * (1.0 / total) - gb + DIAG_SHIFT * cb

    def inner(ua, ub, va, vb):
        return jnp.sum(ua * va + ub * vb, axis=1, keepdims=True)

    mean_re = jnp.sum(a_re, axis=1, keepdims=True) * (1.0 / block)
    mean_im = jnp.sum(a_im, axis=1, keepdims=True) * (1.0 / block)
    da, db = a_re - mean_re, a_im - mean_im
    scalars = [
        inner(ca, cb, a_re, a_im),
        inner(ha, hb, a_re, a_im),
        inner(da, db, da, db),
        mean_re,
        mean_im,
    ]
    s_msg[...] = pack_rows([jnp.broadcast_to(x, (1, 128)) for x in scalars], 8)
    spread(*plane, w, s_msg, s_buf, s_send, s_recv)
    a_mine = piece(pack_rows([a_re, a_im], 8), z)

    for copy in w2_copies:
        copy.wait_send()

    def e_drain(d, carry):
        e_copy(d).wait_send()
        return carry

    lax.fori_loop(1, LINE * pn, e_drain, 0)
    drain(*plane, w, occ_mine, occ_plane, op_send, op_recv)
    drain(*line, z, occ_mine, occ_line, ol_send, ol_recv)
    drain(*plane, w, kp_msg, kp_buf, kp_send, kp_recv)
    drain(*line, z, kl_msg, kl_buf, kl_send, kl_recv)
    drain(*plane, w, y_msg, y_buf, y_send, y_recv)
    drain(*line, z, z_msg, z_buf, z_send, z_recv)

    collect(*plane, s_msg, s_buf, s_send, s_recv)
    s = total_of(s_buf)
    means = s * (1.0 / PLANE)
    spread_sq = jnp.square(s_buf[0] - means)
    for j in range(1, PLANE):
        spread_sq = spread_sq + jnp.square(s_buf[j] - means)
    f_af, af_af = s[0:1, 0:1], s[1:2, 0:1]
    centered = s[2:3, 0:1] + float(block) * (spread_sq[3:4, 0:1] + spread_sq[4:5, 0:1])
    af_aaf = centered * (1.0 / total) + DIAG_SHIFT * af_af
    alpha0 = ff / f_af
    rr = ff - 2.0 * alpha0 * f_af + alpha0 * alpha0 * af_af
    beta = rr / ff
    near = 1.0 + beta
    curv = near * near * f_af - 2.0 * near * alpha0 * af_af + alpha0 * alpha0 * af_aaf
    alpha1 = rr / curv
    on_f = alpha0 + alpha1 * near
    on_af = alpha1 * alpha0
    out_ref[2:3] = on_f * (f_mine[0:1] - f_mean_re) - on_af * (a_mine[0:1] - means[3:4, 0:1])
    out_ref[3:4] = on_f * (f_mine[1:2] - f_mean_im) - on_af * (a_mine[1:2] - means[4:5, 0:1])
    drain(*plane, w, s_msg, s_buf, s_send, s_recv)


def body(occ, counts, orb, elem, step, w1, bias, w2, readout):
    samples = occ.shape[0]
    slots = orb.shape[1]
    depth, hid2 = w2.shape
    hid = w1.shape[1]
    block = LINE * samples
    vmem = pl.BlockSpec(memory_space=pltpu.VMEM)
    hbm = pl.BlockSpec(memory_space=pltpu.HBM)
    dma = pltpu.SemaphoreType.DMA
    inputs = (
        occ,
        counts.reshape(1, samples),
        orb,
        elem,
        step.reshape(1, 1),
        w1,
        bias.reshape(1, hid),
        w2,
        readout,
    )

    def message(n, width):
        return [pltpu.VMEM((8, width), F32), pltpu.VMEM((n, 8, width), F32)]

    out = pl.pallas_call(
        kernel,
        out_shape=jax.ShapeDtypeStruct((4, 128), F32),
        in_specs=[hbm] * 9,
        out_specs=vmem,
        scratch_shapes=[
            *[pltpu.VMEM(x.shape, x.dtype) for x in inputs],
            dma((9,)),
            pltpu.VMEM((samples, 256), BF16),
            pltpu.VMEM((LINE, samples, 256), BF16),
            pltpu.VMEM((PLANE, samples, 256), BF16),
            pltpu.VMEM((depth * PARAMS, hid2), BF16),
            pltpu.VMEM((slots, hid), BF16),
            pltpu.VMEM((slots, samples), BF16),
            pltpu.VMEM((3, block, block), BF16),
            pltpu.VMEM((3, block, block), BF16),
            *message(LINE * PARAMS, 128),
            *message(PLANE, block),
            *message(LINE, block),
            *message(PLANE, block),
            *message(LINE, block),
            *message(PLANE, 128),
            pltpu.VMEM((block // 128, 8, 128), F32),
            dma((5,)),
            dma((5,)),
            *[dma((n,)) for n in (8, 8, 8, 8, 32, 32, 8, 8, 8, 8, 8, 8, 8, 8, 8, 8)],
        ],
        compiler_params=pltpu.CompilerParams(
            collective_id=0, has_side_effects=True, vmem_limit_bytes=61 * 1024 * 1024
        ),
    )(*inputs)
    return out[0:2, :samples], out[2:4, :samples]


def solution(mesh):
    return jax.shard_map(
        body,
        mesh=mesh,
        in_specs=(
            P("samples", None),
            P("samples"),
            P(None, ("samples", "params")),
            P(None, ("samples", "params")),
            P(),
            P(),
            P(),
            P("params", None),
            P(),
        ),
        out_specs=(P(None, "samples"), P(None, "samples")),
        check_vma=False,
    )
```

```python
import jax
import jax.numpy as jnp
from jax import lax
from jax.experimental import pallas as pl
from jax.experimental.pallas import tpu as pltpu
from jax.sharding import PartitionSpec as P

FIELD_SCALE = 0.8
FIELD_RATE = 0.0123
DIAG_SHIFT = 0.01
LINE = 8
PLANE = 8
PARAMS = 4
MESH = pl.DeviceIdType.MESH
F32 = jnp.float32
BF16 = jnp.bfloat16


def sincos(x):
    n = jnp.floor(x * 0.6366197723675814 + 0.5)
    r = x - n * 1.5703125
    r = r - n * 4.8351287841796875e-4
    r = r - n * 3.1385570764541626e-7
    r = r - n * 6.0771005065061922e-11
    z = r * r
    s = r + r * z * (-1.6666654611e-1 + z * (8.3321608736e-3 - z * 1.9515295891e-4))
    c = 1.0 - 0.5 * z + z * z * (
        4.166664568298827e-2 + z * (-1.388731625493765e-3 + z * 2.443315711809948e-5)
    )
    quad = n - 4.0 * jnp.floor(n * 0.25)
    odd = (quad == 1.0) | (quad == 3.0)
    sin = jnp.where(odd, c, s)
    cos = jnp.where(odd, s, c)
    sin = jnp.where(quad >= 2.0, -sin, sin)
    cos = jnp.where((quad == 1.0) | (quad == 2.0), -cos, cos)
    return sin, cos


def parts3(x):
    hi = x.astype(BF16).astype(F32)
    rest = x - hi
    mid = rest.astype(BF16).astype(F32)
    return hi, mid, rest - mid


def pack_rows(rows, height):
    width = rows[0].shape[1]
    place = lax.broadcasted_iota(jnp.int32, (height, width), 0)
    out = jnp.zeros((height, width), F32)
    for i, row in enumerate(rows):
        out = jnp.where(place == i, jnp.broadcast_to(row, (height, width)), out)
    return out


def nn(a, b):
    return lax.dot_general(a, b, (((1,), (0,)), ((), ())), preferred_element_type=F32)


def nt(a, b):
    return lax.dot_general(a, b, (((1,), (1,)), ((), ())), preferred_element_type=F32)


def tn(a, b):
    return lax.dot_general(a, b, (((0,), (0,)), ((), ())), preferred_element_type=F32)


def kernel(
    occ_hbm,
    counts_hbm,
    orb_hbm,
    elem_hbm,
    step_hbm,
    w1_hbm,
    bias_hbm,
    w2_hbm,
    readout_hbm,
    out_ref,
    occ_ref,
    counts_ref,
    orb_ref,
    elem_ref,
    step_ref,
    w1_ref,
    bias_ref,
    w2_ref,
    readout_ref,
    in_sem,
    occ_mine,
    occ_line,
    occ_plane,
    w2_full,
    slot_hid,
    pick,
    pick_t,
    kt_hi,
    kt_lo,
    kr_hi,
    kr_lo,
    e_msg,
    e_buf,
    kp_msg,
    kp_buf,
    kl_msg,
    kl_buf,
    y_msg,
    y_buf,
    z_msg,
    z_buf,
    s_msg,
    s_buf,
    own_buf,
    w2_send,
    w2_recv,
    op_send,
    op_recv,
    ol_send,
    ol_recv,
    e_send,
    e_recv,
    kp_send,
    kp_recv,
    kl_send,
    kl_recv,
    y_send,
    y_recv,
    z_send,
    z_recv,
    s_send,
    s_recv,
):
    outside = (occ_hbm, w2_hbm, w1_hbm, orb_hbm, counts_hbm, bias_hbm, elem_hbm, step_hbm, readout_hbm)
    inside = (occ_ref, w2_ref, w1_ref, orb_ref, counts_ref, bias_ref, elem_ref, step_ref, readout_ref)
    loads = [pltpu.make_async_copy(a, c, in_sem.at[i]) for i, (a, c) in enumerate(zip(outside, inside))]
    for load in loads:
        load.start()
    samples, orbitals = occ_ref.shape
    slots = orb_ref.shape[1]
    depth = w2_ref.shape[0]
    pn = PARAMS
    block = LINE * samples
    total = float(block * PLANE)

    b = lax.axis_index("samples")
    p = lax.axis_index("params")
    z = b // PLANE
    w = b % PLANE
    p_core = p + 1 - 2 * (p % 2)
    p_far = p + 2 - 4 * (p // 2)
    p_cross = p_far + 1 - 2 * (p_far % 2)
    b_pair = b + 1 - 2 * (b % 2)

    def line_peer(d):
        to = lax.rem(z + d, LINE)
        return to, (to * PLANE + w, p)

    def plane_peer(d):
        y, half = w // 2, w % 2
        to_y = lax.rem(y + d // 2, PLANE // 2)
        if d % 2:
            to = to_y * 2 + 1 - half
            return to, (z * PLANE + to, p_far)
        to = to_y * 2 + half
        return to, (z * PLANE + to, p)

    LINE_ORDER = (4, 3, 5, 2, 6, 1, 7)
    PLANE_ORDER = (5, 4, 3, 7, 2, 6, 1)

    def energy_peer(d):
        return lax.rem(z + d // pn, LINE) * PLANE + w, lax.rem(p + lax.rem(d, pn), pn)

    def copy_to(src, dst, send, recv, device):
        return pltpu.make_async_remote_copy(
            src_ref=src, dst_ref=dst, send_sem=send, recv_sem=recv, device_id=device, device_id_type=MESH
        )

    def spread(peer, order, me, msg, buf, send, recv):
        for d in order:
            copy_to(msg, buf.at[me], send.at[d], recv.at[me], peer(d)[1]).start()
        buf[me] = msg[...]

    def collect(peer, order, msg, buf, send, recv):
        for d in order:
            place, device = peer(d)
            copy_to(msg, buf.at[place], send.at[d], recv.at[place], device).wait_recv()

    def drain(peer, order, me, msg, buf, send, recv):
        for d in order:
            copy_to(msg, buf.at[me], send.at[d], recv.at[me], peer(d)[1]).wait_send()

    line = (line_peer, LINE_ORDER)
    plane = (plane_peer, PLANE_ORDER)

    barrier = pltpu.get_barrier_semaphore()

    def signal(device):
        pl.semaphore_signal(barrier, inc=1, device_id=device, device_id_type=MESH)

    signal((b_pair, p_cross))
    for d in PLANE_ORDER:
        signal(plane_peer(d)[1])

    def greet(d, carry):
        signal(energy_peer(d))
        return carry

    lax.fori_loop(1, LINE * pn, greet, 0)

    pl.semaphore_wait(barrier, LINE * pn - 1 + PLANE - 1 + 1)

    half = depth // 2
    whole = pl.ds(pl.multiple_of(p * depth, depth), depth)
    w2_copies = []
    for d, far in ((0, p_far), (1, p_cross)):
        for h, to in ((0, b), (1, b_pair)):
            rows = pl.ds(pl.multiple_of(p * depth + h * half, half), half)
            i = 1 + d * 2 + h
            w2_copies.append(
                copy_to(w2_hbm.at[pl.ds(h * half, half)], w2_full.at[rows], w2_send.at[i], w2_recv.at[i], (to, far))
            )
    w2_copies.append(copy_to(w2_hbm, w2_full.at[whole], w2_send.at[0], w2_recv.at[0], (b, p_core)))
    for copy in w2_copies:
        copy.start()

    loads[0].wait()
    occ = occ_ref[...].astype(F32)
    occ_mine[...] = jnp.zeros_like(occ_mine)
    occ_mine[:, :orbitals] = occ.astype(BF16)
    spread(*plane, w, occ_mine, occ_plane, op_send, op_recv)
    spread(*line, z, occ_mine, occ_line, ol_send, ol_recv)
    loads[1].wait()
    w2_full[whole] = w2_ref[...]

    for load in loads[2:]:
        load.wait()
    counts = jnp.broadcast_to(counts_ref[...].astype(F32), (8, samples))
    r_id = lax.broadcasted_iota(jnp.int32, (samples, samples), 0)
    c_id = lax.broadcasted_iota(jnp.int32, (samples, samples), 1)
    upto = (r_id <= c_id).astype(BF16)
    c_hi, c_mid, c_lo = parts3(counts)
    ends = nn(c_hi.astype(BF16), upto) + nn(c_mid.astype(BF16), upto) + nn(c_lo.astype(BF16), upto)
    begins = ends - counts
    position = (p + pn * lax.broadcasted_iota(jnp.int32, (slots, samples), 0)).astype(F32)
    pick[...] = ((begins[0:1] <= position) & (position < ends[0:1])).astype(BF16)
    ends_col, begins_col = ends.T[:, 0:1], begins.T[:, 0:1]
    position = (p + pn * lax.broadcasted_iota(jnp.int32, (samples, slots), 1)).astype(F32)
    pick_t[...] = ((begins_col <= position) & (position < ends_col)).astype(BF16)
    ends = ends[0:1]
    occ_t = occ.T.astype(BF16)
    w1 = w1_ref[...]
    bias = bias_ref[...]
    chunk = 256
    for start_row in range(0, slots, chunk):
        rows = slice(start_row, start_row + chunk)
        base = nn(occ_t, pick_t[:, rows])
        column = lax.broadcasted_iota(jnp.int32, (orbitals, chunk), 0)
        orb = orb_ref[:, rows]
        flip = orb[0:1] == column
        for u in range(1, orb_ref.shape[0]):
            flip = flip | (orb[u : u + 1] == column)
        flipped = jnp.where(flip, 1.0 - base, base).astype(BF16)
        slot_hid[rows] = jnp.tanh(tn(flipped, w1) + bias).astype(BF16)
    hidden = jnp.tanh(nn(occ_mine[:, :orbitals], w1) + bias).astype(BF16)

    for copy in w2_copies:
        copy.wait_recv()
    w2 = w2_full[...]

    readout = readout_ref[...]
    r_rows = pack_rows([x[i : i + 1] for x in parts3(readout) for i in range(2)], 128)
    r_cols = r_rows.T.astype(BF16)

    def logs_of(hid):
        mid = jnp.tanh(nn(hid, w2))
        hi = mid.astype(BF16)
        lo = (mid - hi.astype(F32)).astype(BF16)
        out = (nn(hi, r_cols) + nn(lo, r_cols)).T
        return out[0:2] + out[2:4] + out[4:6]

    logs = logs_of(hidden)
    slot_logs = logs_of(slot_hid[...])
    l_rows = pack_rows([x[i : i + 1] for x in parts3(logs) for i in range(2)], 16).astype(BF16)
    parent_logs = nn(l_rows, pick_t[...])
    parent_logs = parent_logs[0:2] + parent_logs[2:4] + parent_logs[4:6]
    diff = slot_logs - parent_logs
    angle = jnp.broadcast_to(step_ref[...].astype(F32), (1, slots)) * FIELD_RATE
    field = FIELD_SCALE * sincos(angle)[0]
    elem = elem_ref[...]
    weight = elem[0:1] + field * elem[1:2]
    slot_at = (p + pn * lax.broadcasted_iota(jnp.int32, (1, slots), 1)).astype(F32)
    used = slot_at < ends[0:1, samples - 1 : samples]
    size = jnp.exp(diff[0:1])
    sin, cos = sincos(diff[1:2])
    contrib = [jnp.where(used, weight * (size * cos), 0.0), jnp.where(used, weight * (size * sin), 0.0)]
    splits = [parts3(x) for x in contrib]
    e_rows = pack_rows([splits[i][j] for j in range(3) for i in range(2)], 16).astype(BF16)
    energy = nn(e_rows, pick[...])
    energy = energy[0:2] + energy[2:4] + energy[4:6]
    e_msg[...] = jnp.zeros_like(e_msg)
    e_msg[0:2, :samples] = energy

    me = z * pn + p

    def e_copy(d):
        return copy_to(e_msg, e_buf.at[me], e_send.at[d], e_recv.at[me], energy_peer(d))

    for dz in (*LINE_ORDER, 0):
        for dp in range(pn):
            if dz * pn + dp:
                e_copy(dz * pn + dp).start()
    e_buf[me] = e_msg[...]

    collect(*plane, occ_mine, occ_plane, op_send, op_recv)
    collect(*line, occ_mine, occ_line, ol_send, ol_recv)

    def hidden_of(ref):
        rows = ref[...].reshape(block, ref.shape[2])[:, :orbitals]
        return jnp.tanh(nn(rows, w1) + bias).astype(BF16)

    def slope_of(hid):
        mid = jnp.tanh(nn(hid, w2))
        return 1.0 - mid * mid

    hid_c = hidden_of(occ_line)
    hid_r = hidden_of(occ_plane)
    slope_c = slope_of(hid_c)
    slope_r = slope_of(hid_r)
    gram = nt(hid_c, hid_r)
    r_hi = slope_r.astype(BF16)
    r_lo = (slope_r - r_hi.astype(F32)).astype(BF16)
    ones_r, ones_c = [], []
    pairs = (readout[0:1] * readout[0:1], readout[0:1] * readout[1:2], readout[1:2] * readout[1:2])
    for t, pair in enumerate(pairs):
        scaled = slope_c * pair
        s_hi = scaled.astype(BF16)
        s_lo = (scaled - s_hi.astype(F32)).astype(BF16)
        kt = gram * (nt(s_hi, r_hi) + (nt(s_lo, r_hi) + nt(s_hi, r_lo)))
        hi = kt.astype(BF16)
        lo = (kt - hi.astype(F32)).astype(BF16)
        kt_hi[t] = hi
        kt_lo[t] = lo
        ones_r.append(jnp.sum(kt, axis=0, keepdims=True))
        turned = kt.T
        hi = turned.astype(BF16)
        kr_hi[t] = hi
        kr_lo[t] = (turned - hi.astype(F32)).astype(BF16)
        ones_c.append(jnp.sum(turned, axis=0, keepdims=True))
    kp_msg[...] = pack_rows(ones_r, 8)
    kl_msg[...] = pack_rows(ones_c, 8)
    spread(*plane, w, kp_msg, kp_buf, kp_send, kp_recv)
    spread(*line, z, kl_msg, kl_buf, kl_send, kl_recv)

    def apply(va, vb, ones, k_hi, k_lo):
        ma = jnp.sum(va, axis=1, keepdims=True) * (1.0 / block)
        mb = jnp.sum(vb, axis=1, keepdims=True) * (1.0 / block)
        rows = pack_rows([*parts3(va - ma), *parts3(vb - mb)], 16).astype(BF16)
        outs = []
        for t in range(3):
            out = nn(rows, k_hi[t]) + nn(rows, k_lo[t])
            outs.append((out[0:1] + out[1:2] + out[2:3], out[3:4] + out[4:5] + out[5:6]))
        y_re = outs[0][0] + outs[1][1] + (ones[0] * ma + ones[1] * mb)
        y_im = outs[1][0] + outs[2][1] + (ones[1] * ma + ones[2] * mb)
        return y_re, y_im

    def total_of(buf):
        acc = buf[0]
        for j in range(1, buf.shape[0]):
            acc = acc + buf[j]
        return acc

    def pieces(tiles):
        pairs = [tiles[i] + pltpu.roll(tiles[i + 1], samples, 1) for i in range(0, len(tiles), 2)]
        return jnp.concatenate(pairs, axis=1)

    lane = lax.broadcasted_iota(jnp.int32, (8, 128), 1)

    def piece(value, place):
        for i in range(block // 128):
            own_buf[i] = value[:, i * 128 : (i + 1) * 128]
        tile = own_buf[place // 2]
        odd = jnp.full(tile.shape, place % 2, jnp.int32) == 1
        tile = jnp.where(odd, pltpu.roll(tile, samples, 1), tile)
        return jnp.where(lane < samples, tile, 0.0)

    def e_wait(d, carry):
        to_b, to_p = energy_peer(d)
        place = (to_b // PLANE) * pn + to_p
        copy_to(e_msg, e_buf.at[place], e_send.at[d], e_recv.at[place], (to_b, to_p)).wait_recv()
        return carry

    lax.fori_loop(1, LINE * pn, e_wait, 0)

    def over_params(i):
        acc = e_buf[i * pn]
        for j in range(1, pn):
            acc = acc + e_buf[i * pn + j]
        return acc

    energies = pieces([over_params(i) for i in range(LINE)])
    mine = over_params(z)
    out_ref[0:2] = mine[0:2]

    ea = energies[1:2] * (1.0 / total)
    eb = energies[0:1] * (-1.0 / total)
    y_re, y_im = apply(ea, eb, ones_r, kt_hi, kt_lo)
    y_msg[0:8] = pack_rows([y_re, y_im], 8)
    y_msg[2:4, 0:128] = mine[0:2]
    means = [jnp.sum(v, axis=1, keepdims=True) * (1.0 / total) for v in (ea, eb)]
    y_msg[2:4, 128:256] = pack_rows([jnp.broadcast_to(v, (1, 128)) for v in means], 2)
    spread(*plane, w, y_msg, y_buf, y_send, y_recv)
    collect(*plane, kp_msg, kp_buf, kp_send, kp_recv)
    collect(*plane, y_msg, y_buf, y_send, y_recv)
    k1 = total_of(kp_buf)
    y = total_of(y_buf)
    ga, gb = y[2:3, 128:129], y[3:4, 128:129]
    around = pieces([y_buf[i, :, 0:128] for i in range(PLANE)])
    fa = around[3:4] * (1.0 / total) - ga
    fb = around[2:3] * (-1.0 / total) - gb
    f_re = y[0:1] - (k1[0:1] * ga + k1[1:2] * gb)
    f_im = y[1:2] - (k1[1:2] * ga + k1[2:3] * gb)

    ha = f_re * (1.0 / total) + DIAG_SHIFT * fa
    hb = f_im * (1.0 / total) + DIAG_SHIFT * fb
    z_re, z_im = apply(ha, hb, ones_c, kr_hi, kr_lo)
    z_msg[0:8] = pack_rows([z_re, z_im], 8)
    f_mine = piece(pack_rows([f_re, f_im], 8), w)
    z_msg[2:4, 0:128] = f_mine[0:2]
    norm = jnp.sum(fa * f_re + fb * f_im, axis=1, keepdims=True)
    means = [jnp.sum(v, axis=1, keepdims=True) * (1.0 / total) for v in (f_re, f_im)]
    z_msg[2:5, 128:256] = pack_rows([jnp.broadcast_to(v, (1, 128)) for v in (*means, norm)], 3)
    spread(*line, z, z_msg, z_buf, z_send, z_recv)
    ca, cb = ea - ga, eb - gb
    collect(*line, kl_msg, kl_buf, kl_send, kl_recv)
    collect(*line, z_msg, z_buf, z_send, z_recv)
    k1 = total_of(kl_buf)
    acc = total_of(z_buf)
    f_mean_re, f_mean_im, ff = acc[2:3, 128:129], acc[3:4, 128:129], acc[4:5, 128:129]
    ga, gb = f_mean_re * (1.0 / total), f_mean_im * (1.0 / total)
    a_re = acc[0:1] - (k1[0:1] * ga + k1[1:2] * gb)
    a_im = acc[1:2] - (k1[1:2] * ga + k1[2:3] * gb)
    along = pieces([z_buf[i, :, 0:128] for i in range(LINE)])
    ha = along[2:3] * (1.0 / total) - ga + DIAG_SHIFT * ca
    hb = along[3:4] * (1.0 / total) - gb + DIAG_SHIFT * cb

    def inner(ua, ub, va, vb):
        return jnp.sum(ua * va + ub * vb, axis=1, keepdims=True)

    mean_re = jnp.sum(a_re, axis=1, keepdims=True) * (1.0 / block)
    mean_im = jnp.sum(a_im, axis=1, keepdims=True) * (1.0 / block)
    da, db = a_re - mean_re, a_im - mean_im
    scalars = [
        inner(ca, cb, a_re, a_im),
        inner(ha, hb, a_re, a_im),
        inner(da, db, da, db),
        mean_re,
        mean_im,
    ]
    s_msg[...] = pack_rows([jnp.broadcast_to(x, (1, 128)) for x in scalars], 8)
    spread(*plane, w, s_msg, s_buf, s_send, s_recv)
    a_mine = piece(pack_rows([a_re, a_im], 8), z)

    for copy in w2_copies:
        copy.wait_send()

    def e_drain(d, carry):
        e_copy(d).wait_send()
        return carry

    lax.fori_loop(1, LINE * pn, e_drain, 0)
    drain(*plane, w, occ_mine, occ_plane, op_send, op_recv)
    drain(*line, z, occ_mine, occ_line, ol_send, ol_recv)
    drain(*plane, w, kp_msg, kp_buf, kp_send, kp_recv)
    drain(*line, z, kl_msg, kl_buf, kl_send, kl_recv)
    drain(*plane, w, y_msg, y_buf, y_send, y_recv)
    drain(*line, z, z_msg, z_buf, z_send, z_recv)

    collect(*plane, s_msg, s_buf, s_send, s_recv)
    s = total_of(s_buf)
    means = s * (1.0 / PLANE)
    spread_sq = jnp.square(s_buf[0] - means)
    for j in range(1, PLANE):
        spread_sq = spread_sq + jnp.square(s_buf[j] - means)
    f_af, af_af = s[0:1, 0:1], s[1:2, 0:1]
    centered = s[2:3, 0:1] + float(block) * (spread_sq[3:4, 0:1] + spread_sq[4:5, 0:1])
    af_aaf = centered * (1.0 / total) + DIAG_SHIFT * af_af
    alpha0 = ff / f_af
    rr = ff - 2.0 * alpha0 * f_af + alpha0 * alpha0 * af_af
    beta = rr / ff
    near = 1.0 + beta
    curv = near * near * f_af - 2.0 * near * alpha0 * af_af + alpha0 * alpha0 * af_aaf
    alpha1 = rr / curv
    on_f = alpha0 + alpha1 * near
    on_af = alpha1 * alpha0
    out_ref[2:3] = on_f * (f_mine[0:1] - f_mean_re) - on_af * (a_mine[0:1] - means[3:4, 0:1])
    out_ref[3:4] = on_f * (f_mine[1:2] - f_mean_im) - on_af * (a_mine[1:2] - means[4:5, 0:1])
    drain(*plane, w, s_msg, s_buf, s_send, s_recv)


def body(occ, counts, orb, elem, step, w1, bias, w2, readout):
    samples = occ.shape[0]
    slots = orb.shape[1]
    depth, hid2 = w2.shape
    hid = w1.shape[1]
    block = LINE * samples
    vmem = pl.BlockSpec(memory_space=pltpu.VMEM)
    hbm = pl.BlockSpec(memory_space=pltpu.HBM)
    dma = pltpu.SemaphoreType.DMA
    inputs = (
        occ,
        counts.reshape(1, samples),
        orb,
        elem,
        step.reshape(1, 1),
        w1,
        bias.reshape(1, hid),
        w2,
        readout,
    )

    def message(n, width):
        return [pltpu.VMEM((8, width), F32), pltpu.VMEM((n, 8, width), F32)]

    out = pl.pallas_call(
        kernel,
        out_shape=jax.ShapeDtypeStruct((4, 128), F32),
        in_specs=[hbm] * 9,
        out_specs=vmem,
        scratch_shapes=[
            *[pltpu.VMEM(x.shape, x.dtype) for x in inputs],
            dma((9,)),
            pltpu.VMEM((samples, 256), BF16),
            pltpu.VMEM((LINE, samples, 256), BF16),
            pltpu.VMEM((PLANE, samples, 256), BF16),
            pltpu.VMEM((depth * PARAMS, hid2), BF16),
            pltpu.VMEM((slots, hid), BF16),
            pltpu.VMEM((slots, samples), BF16),
            pltpu.VMEM((samples, slots), BF16),
            *[pltpu.VMEM((3, block, block), BF16)] * 4,
            *message(LINE * PARAMS, 128),
            *message(PLANE, block),
            *message(LINE, block),
            *message(PLANE, block),
            *message(LINE, block),
            *message(PLANE, 128),
            pltpu.VMEM((block // 128, 8, 128), F32),
            dma((5,)),
            dma((5,)),
            *[dma((n,)) for n in (8, 8, 8, 8, 32, 32, 8, 8, 8, 8, 8, 8, 8, 8, 8, 8)],
        ],
        compiler_params=pltpu.CompilerParams(
            collective_id=0, has_side_effects=True, vmem_limit_bytes=61 * 1024 * 1024
        ),
    )(*inputs)
    return out[0:2, :samples], out[2:4, :samples]


def solution(mesh):
    return jax.shard_map(
        body,
        mesh=mesh,
        in_specs=(
            P("samples", None),
            P("samples"),
            P(None, ("samples", "params")),
            P(None, ("samples", "params")),
            P(),
            P(),
            P(),
            P("params", None),
            P(),
        ),
        out_specs=(P(None, "samples"), P(None, "samples")),
        check_vma=False,
    )
```

```python
import jax
import jax.numpy as jnp
from jax import lax
from jax.experimental import pallas as pl
from jax.experimental.pallas import tpu as pltpu
from jax.sharding import PartitionSpec as P

FIELD_SCALE = 0.8
FIELD_RATE = 0.0123
DIAG_SHIFT = 0.01
LINE = 8
PLANE = 8
PARAMS = 4
MESH = pl.DeviceIdType.MESH
F32 = jnp.float32
BF16 = jnp.bfloat16


def sincos(x):
    n = jnp.floor(x * 0.6366197723675814 + 0.5)
    r = x - n * 1.5703125
    r = r - n * 4.8351287841796875e-4
    r = r - n * 3.1385570764541626e-7
    r = r - n * 6.0771005065061922e-11
    z = r * r
    s = r + r * z * (-1.6666654611e-1 + z * (8.3321608736e-3 - z * 1.9515295891e-4))
    c = 1.0 - 0.5 * z + z * z * (
        4.166664568298827e-2 + z * (-1.388731625493765e-3 + z * 2.443315711809948e-5)
    )
    quad = n - 4.0 * jnp.floor(n * 0.25)
    odd = (quad == 1.0) | (quad == 3.0)
    sin = jnp.where(odd, c, s)
    cos = jnp.where(odd, s, c)
    sin = jnp.where(quad >= 2.0, -sin, sin)
    cos = jnp.where((quad == 1.0) | (quad == 2.0), -cos, cos)
    return sin, cos


def parts3(x):
    hi = x.astype(BF16).astype(F32)
    rest = x - hi
    mid = rest.astype(BF16).astype(F32)
    return hi, mid, rest - mid


def pack_rows(rows, height):
    width = rows[0].shape[1]
    place = lax.broadcasted_iota(jnp.int32, (height, width), 0)
    out = jnp.zeros((height, width), F32)
    for i, row in enumerate(rows):
        out = jnp.where(place == i, jnp.broadcast_to(row, (height, width)), out)
    return out


def nn(a, b):
    return lax.dot_general(a, b, (((1,), (0,)), ((), ())), preferred_element_type=F32)


def nt(a, b):
    return lax.dot_general(a, b, (((1,), (1,)), ((), ())), preferred_element_type=F32)


def tn(a, b):
    return lax.dot_general(a, b, (((0,), (0,)), ((), ())), preferred_element_type=F32)


def kernel(
    occ_hbm,
    counts_hbm,
    orb_hbm,
    elem_hbm,
    step_hbm,
    w1_hbm,
    bias_hbm,
    w2_hbm,
    readout_hbm,
    out_ref,
    occ_ref,
    counts_ref,
    orb_ref,
    elem_ref,
    step_ref,
    w1_ref,
    bias_ref,
    w2_ref,
    readout_ref,
    in_sem,
    occ_mine,
    occ_line,
    occ_plane,
    w2_full,
    slot_hid,
    pick,
    pick_t,
    hid_plane,
    slope_plane,
    kt_full,
    kt_hi,
    kt_lo,
    kr_hi,
    kr_lo,
    e_msg,
    e_buf,
    kp_msg,
    kp_buf,
    kl_msg,
    kl_buf,
    yx_msg,
    yx_buf,
    y_msg,
    y_buf,
    zx_msg,
    zx_buf,
    z_msg,
    z_buf,
    s_msg,
    s_buf,
    own_buf,
    w2_send,
    w2_recv,
    op_send,
    op_recv,
    ol_send,
    ol_recv,
    share_send,
    share_recv,
    e_send,
    e_recv,
    kp_send,
    kp_recv,
    kl_send,
    kl_recv,
    yx_send,
    yx_recv,
    y_send,
    y_recv,
    zx_send,
    zx_recv,
    z_send,
    z_recv,
    s_send,
    s_recv,
):
    outside = (occ_hbm, w2_hbm, w1_hbm, orb_hbm, counts_hbm, bias_hbm, elem_hbm, step_hbm, readout_hbm)
    inside = (occ_ref, w2_ref, w1_ref, orb_ref, counts_ref, bias_ref, elem_ref, step_ref, readout_ref)
    loads = [pltpu.make_async_copy(a, c, in_sem.at[i]) for i, (a, c) in enumerate(zip(outside, inside))]
    samples, orbitals = occ_ref.shape
    slots = orb_ref.shape[1]
    depth = w2_ref.shape[0]
    pn = PARAMS
    block = LINE * samples
    total = float(block * PLANE)

    b = lax.axis_index("samples")
    p = lax.axis_index("params")
    z = b // PLANE
    w = b % PLANE
    p_core = p + 1 - 2 * (p % 2)
    p_far = p + 2 - 4 * (p // 2)
    p_cross = p_far + 1 - 2 * (p_far % 2)
    b_pair = b + 1 - 2 * (b % 2)

    def line_peer(d):
        to = lax.rem(z + d, LINE)
        return to, (to * PLANE + w, p)

    def plane_peer(d):
        y, half = w // 2, w % 2
        to_y = lax.rem(y + d // 2, PLANE // 2)
        if d % 2:
            to = to_y * 2 + 1 - half
            return to, (z * PLANE + to, p_far)
        to = to_y * 2 + half
        return to, (z * PLANE + to, p)

    LINE_ORDER = (4, 3, 5, 2, 6, 1, 7)
    PLANE_ORDER = (5, 4, 3, 7, 2, 6, 1)

    def energy_peer(d):
        return lax.rem(z + d // pn, LINE) * PLANE + w, lax.rem(p + lax.rem(d, pn), pn)

    def copy_to(src, dst, send, recv, device):
        return pltpu.make_async_remote_copy(
            src_ref=src, dst_ref=dst, send_sem=send, recv_sem=recv, device_id=device, device_id_type=MESH
        )

    def spread(peer, order, me, msg, buf, send, recv, keep=True):
        for d in order:
            copy_to(msg, buf.at[me], send.at[d], recv.at[me], peer(d)[1]).start()
        if keep:
            buf[me] = msg[...]

    def collect(peer, order, msg, buf, send, recv):
        for d in order:
            place, device = peer(d)
            copy_to(msg, buf.at[place], send.at[d], recv.at[place], device).wait_recv()

    def drain(peer, order, me, msg, buf, send, recv):
        for d in order:
            copy_to(msg, buf.at[me], send.at[d], recv.at[me], peer(d)[1]).wait_send()

    line = (line_peer, LINE_ORDER)
    plane = (plane_peer, PLANE_ORDER)

    barrier = pltpu.get_barrier_semaphore()

    def signal(device):
        pl.semaphore_signal(barrier, inc=1, device_id=device, device_id_type=MESH)

    signal((b_pair, p_cross))
    for d in PLANE_ORDER:
        signal(plane_peer(d)[1])

    for dz in (0, *LINE_ORDER):
        to_b = lax.rem(z + dz, LINE) * PLANE + w
        for dp in range(pn):
            if dz or dp:
                signal((to_b, lax.rem(p + dp, pn)))
    for load in loads:
        load.start()

    loads[0].wait()
    occ = occ_ref[...].astype(F32)
    occ_mine[...] = jnp.zeros_like(occ_mine)
    core = p % 2
    rows_here = samples // 2
    for h in range(2):
        occ_mine[h, :, :orbitals] = occ[h * rows_here : (h + 1) * rows_here].astype(BF16)
    pl.semaphore_wait(barrier, LINE * pn - 1 + PLANE - 1 + 1)

    spread(*line, z, occ_mine.at[core], occ_line.at[core], ol_send, ol_recv, False)
    half = depth // 2
    whole = pl.ds(pl.multiple_of(p * depth, depth), depth)
    w2_copies = []
    for d, far in ((0, p_far), (1, p_cross)):
        for h, to in ((0, b), (1, b_pair)):
            rows = pl.ds(pl.multiple_of(p * depth + h * half, half), half)
            i = 1 + d * 2 + h
            w2_copies.append(
                copy_to(w2_hbm.at[pl.ds(h * half, half)], w2_full.at[rows], w2_send.at[i], w2_recv.at[i], (to, far))
            )
    w2_copies.append(copy_to(w2_hbm, w2_full.at[whole], w2_send.at[0], w2_recv.at[0], (b, p_core)))
    for copy in w2_copies:
        copy.start()

    spread(*plane, w, occ_mine.at[core], occ_plane.at[core], op_send, op_recv, False)
    occ_line[core, z] = occ_mine[core]
    occ_plane[core, w] = occ_mine[core]
    loads[1].wait()
    w2_full[whole] = w2_ref[...]

    for load in loads[2:]:
        load.wait()
    counts = jnp.broadcast_to(counts_ref[...].astype(F32), (8, samples))
    r_id = lax.broadcasted_iota(jnp.int32, (samples, samples), 0)
    c_id = lax.broadcasted_iota(jnp.int32, (samples, samples), 1)
    upto = (r_id <= c_id).astype(BF16)
    c_hi, c_mid, c_lo = parts3(counts)
    ends = nn(c_hi.astype(BF16), upto) + nn(c_mid.astype(BF16), upto) + nn(c_lo.astype(BF16), upto)
    begins = ends - counts
    position = (p + pn * lax.broadcasted_iota(jnp.int32, (slots, samples), 0)).astype(F32)
    pick[...] = ((begins[0:1] <= position) & (position < ends[0:1])).astype(BF16)
    ends_col, begins_col = ends.T[:, 0:1], begins.T[:, 0:1]
    position = (p + pn * lax.broadcasted_iota(jnp.int32, (samples, slots), 1)).astype(F32)
    pick_t[...] = ((begins_col <= position) & (position < ends_col)).astype(BF16)
    ends = ends[0:1]
    occ_t = occ.T.astype(BF16)
    w1 = w1_ref[...]
    bias = bias_ref[...]
    chunk = 256
    for start_row in range(0, slots, chunk):
        rows = slice(start_row, start_row + chunk)
        base = nn(occ_t, pick_t[:, rows])
        column = lax.broadcasted_iota(jnp.int32, (orbitals, chunk), 0)
        orb = orb_ref[:, rows]
        flip = orb[0:1] == column
        for u in range(1, orb_ref.shape[0]):
            flip = flip | (orb[u : u + 1] == column)
        flipped = jnp.where(flip, 1.0 - base, base).astype(BF16)
        slot_hid[rows] = jnp.tanh(tn(flipped, w1) + bias).astype(BF16)
    hidden = jnp.tanh(nn(occ.astype(BF16), w1) + bias).astype(BF16)

    for copy in w2_copies:
        copy.wait_recv()
    w2 = w2_full[...]
    shares = [
        copy_to(buf.at[core], buf.at[core], share_send.at[i], share_recv.at[i], (b, p_core))
        for i, buf in enumerate((occ_line, occ_plane))
    ]
    collect(*line, occ_mine.at[core], occ_line.at[core], ol_send, ol_recv)
    shares[0].start()

    readout = readout_ref[...]
    r_rows = pack_rows([x[i : i + 1] for x in parts3(readout) for i in range(2)], 128)
    r_cols = r_rows.T.astype(BF16)

    def logs_of(hid):
        mid = jnp.tanh(nn(hid, w2))
        hi = mid.astype(BF16)
        lo = (mid - hi.astype(F32)).astype(BF16)
        out = (nn(hi, r_cols) + nn(lo, r_cols)).T
        return out[0:2] + out[2:4] + out[4:6]

    logs = logs_of(hidden)
    slot_logs = logs_of(slot_hid[...])
    l_rows = pack_rows([x[i : i + 1] for x in parts3(logs) for i in range(2)], 16).astype(BF16)
    parent_logs = nn(l_rows, pick_t[...])
    parent_logs = parent_logs[0:2] + parent_logs[2:4] + parent_logs[4:6]
    diff = slot_logs - parent_logs
    angle = jnp.broadcast_to(step_ref[...].astype(F32), (1, slots)) * FIELD_RATE
    field = FIELD_SCALE * sincos(angle)[0]
    elem = elem_ref[...]
    weight = elem[0:1] + field * elem[1:2]
    slot_at = (p + pn * lax.broadcasted_iota(jnp.int32, (1, slots), 1)).astype(F32)
    used = slot_at < ends[0:1, samples - 1 : samples]
    size = jnp.exp(diff[0:1])
    sin, cos = sincos(diff[1:2])
    contrib = [jnp.where(used, weight * (size * cos), 0.0), jnp.where(used, weight * (size * sin), 0.0)]
    splits = [parts3(x) for x in contrib]
    e_rows = pack_rows([splits[i][j] for j in range(3) for i in range(2)], 16).astype(BF16)
    energy = nn(e_rows, pick[...])
    energy = energy[0:2] + energy[2:4] + energy[4:6]
    e_msg[...] = jnp.concatenate([energy, jnp.zeros((2, 128 - samples), F32)], axis=1)

    me = z * pn + p

    def e_copy(d):
        return copy_to(e_msg, e_buf.at[me], e_send.at[d], e_recv.at[me], energy_peer(d))

    for dz in (*LINE_ORDER, 0):
        for dp in range(pn):
            if dz * pn + dp:
                e_copy(dz * pn + dp).start()
    e_buf[me] = e_msg[...]

    def fold(re, im):
        return pack_rows([row[:, i * 128 : (i + 1) * 128] for row in (re, im) for i in range(block // 128)], 8)

    def unfold(tile):
        n = block // 128
        return [jnp.concatenate([tile[at + i : at + i + 1] for i in range(n)], axis=1) for at in (0, n)]

    def wide(row):
        return jnp.concatenate([row] * (block // 128), axis=1)

    def row_sum(value):
        return jnp.broadcast_to(jnp.sum(value, axis=1, keepdims=True), (1, 128))

    def hidden_of(parts):
        rows = jnp.concatenate(parts, axis=0)[:, :orbitals]
        return jnp.tanh(nn(rows, w1) + bias).astype(BF16)

    def slope_of(hid):
        mid = jnp.tanh(nn(hid, w2))
        return 1.0 - mid * mid

    def half_of_plane(h):
        hid = hidden_of([occ_plane[h, i] for i in range(PLANE)])
        slope = slope_of(hid)
        for i in range(PLANE):
            rows = slice(i * rows_here, (i + 1) * rows_here)
            hid_plane[i, h] = hid[rows]
            slope_plane[i, h] = slope[rows]

    collect(*plane, occ_mine.at[core], occ_plane.at[core], op_send, op_recv)
    shares[1].start()
    shares[0].wait_recv()
    hid_c = hidden_of([occ_line[h, i] for i in range(LINE) for h in range(2)])
    slope_c = slope_of(hid_c)
    half_of_plane(core)
    shares[1].wait_recv()
    half_of_plane(1 - core)
    hid_r = hid_plane[...].reshape(block, hid_plane.shape[3])
    slope_r = slope_plane[...].reshape(block, slope_plane.shape[3])
    gram = nt(hid_c, hid_r)
    r_hi = slope_r.astype(BF16)
    r_lo = (slope_r - r_hi.astype(F32)).astype(BF16)
    ones_r, ones_c = [], []
    pairs = (readout[0:1] * readout[0:1], readout[0:1] * readout[1:2], readout[1:2] * readout[1:2])
    for t, pair in enumerate(pairs):
        scaled = slope_c * pair
        s_hi = scaled.astype(BF16)
        s_lo = (scaled - s_hi.astype(F32)).astype(BF16)
        kt = gram * (nt(s_hi, r_hi) + (nt(s_lo, r_hi) + nt(s_hi, r_lo)))
        hi = kt.astype(BF16)
        lo = (kt - hi.astype(F32)).astype(BF16)
        kt_hi[t] = hi
        kt_lo[t] = lo
        kt_full[t] = kt
        ones_r.append(jnp.sum(kt, axis=0, keepdims=True))
    kp_msg[0:8] = fold(ones_r[0], ones_r[1])
    kp_msg[8:16] = fold(ones_r[1], ones_r[2])
    spread(*plane, w, kp_msg, kp_buf, kp_send, kp_recv)

    def apply(va, vb, ones, k_hi, k_lo):
        ma = jnp.sum(va, axis=1, keepdims=True) * (1.0 / block)
        mb = jnp.sum(vb, axis=1, keepdims=True) * (1.0 / block)
        rows = pack_rows([*parts3(va - ma), *parts3(vb - mb)], 16).astype(BF16)
        outs = []
        for t in range(3):
            out = nn(rows, k_hi[t]) + nn(rows, k_lo[t])
            outs.append((out[0:1] + out[1:2] + out[2:3], out[3:4] + out[4:5] + out[5:6]))
        y_re = outs[0][0] + outs[1][1] + (ones[0] * ma + ones[1] * mb)
        y_im = outs[1][0] + outs[2][1] + (ones[1] * ma + ones[2] * mb)
        return y_re, y_im

    def total_of(buf):
        acc = buf[0]
        for j in range(1, buf.shape[0]):
            acc = acc + buf[j]
        return acc

    def pieces(tiles):
        pairs = [tiles[i] + pltpu.roll(tiles[i + 1], samples, 1) for i in range(0, len(tiles), 2)]
        return jnp.concatenate(pairs, axis=1)

    lane = lax.broadcasted_iota(jnp.int32, (2, 128), 1)

    def piece(tile, place):
        own_buf[...] = tile
        rows = jnp.concatenate([own_buf[pl.ds(place // 2, 1)], own_buf[pl.ds(place // 2 + 4, 1)]], axis=0)
        odd = jnp.full(rows.shape, place % 2, jnp.int32) == 1
        rows = jnp.where(odd, pltpu.roll(rows, samples, 1), rows)
        return jnp.where(lane < samples, rows, 0.0)

    def e_wait(d, carry):
        to_b, to_p = energy_peer(d)
        place = (to_b // PLANE) * pn + to_p
        copy_to(e_msg, e_buf.at[place], e_send.at[d], e_recv.at[place], (to_b, to_p)).wait_recv()
        return carry

    lax.fori_loop(1, LINE * pn, e_wait, 0)

    def over_params(i):
        acc = e_buf[i * pn]
        for j in range(1, pn):
            acc = acc + e_buf[i * pn + j]
        return acc

    energies = pieces([over_params(i) for i in range(LINE)])
    mine = over_params(z)
    out_ref[0:2] = mine

    ea = energies[1:2] * (1.0 / total)
    eb = energies[0:1] * (-1.0 / total)
    yx_msg[0:2] = mine
    yx_msg[2:3] = row_sum(ea) * (1.0 / total)
    yx_msg[3:4] = row_sum(eb) * (1.0 / total)
    spread(*plane, w, yx_msg, yx_buf, yx_send, yx_recv)
    y_msg[...] = fold(*apply(ea, eb, ones_r, kt_hi, kt_lo))
    spread(*plane, w, y_msg, y_buf, y_send, y_recv)
    for t in range(3):
        turned = kt_full[t].T
        hi = turned.astype(BF16)
        kr_hi[t] = hi
        kr_lo[t] = (turned - hi.astype(F32)).astype(BF16)
        ones_c.append(jnp.sum(turned, axis=0, keepdims=True))
    kl_msg[0:8] = fold(ones_c[0], ones_c[1])
    kl_msg[8:16] = fold(ones_c[1], ones_c[2])
    spread(*line, z, kl_msg, kl_buf, kl_send, kl_recv)
    collect(*plane, kp_msg, kp_buf, kp_send, kp_recv)
    k1 = total_of(kp_buf)
    collect(*plane, yx_msg, yx_buf, yx_send, yx_recv)
    means = total_of(yx_buf)
    ga, gb = means[2:3], means[3:4]
    around = pieces([yx_buf[i] for i in range(PLANE)])
    fa = around[1:2] * (1.0 / total) - wide(ga)
    fb = around[0:1] * (-1.0 / total) - wide(gb)
    fix = k1[0:8] * ga + k1[8:16] * gb
    collect(*plane, y_msg, y_buf, y_send, y_recv)
    f_tile = total_of(y_buf) - fix
    f_re, f_im = unfold(f_tile)

    f_mine = piece(f_tile, w)
    zx_msg[0:2] = f_mine
    zx_msg[2:3] = row_sum(f_re) * (1.0 / total)
    zx_msg[3:4] = row_sum(f_im) * (1.0 / total)
    zx_msg[4:5] = row_sum(fa * f_re + fb * f_im)
    zx_msg[5:8] = jnp.zeros((3, 128), F32)
    spread(*line, z, zx_msg, zx_buf, zx_send, zx_recv)
    ha = f_re * (1.0 / total) + DIAG_SHIFT * fa
    hb = f_im * (1.0 / total) + DIAG_SHIFT * fb
    z_msg[...] = fold(*apply(ha, hb, ones_c, kr_hi, kr_lo))
    spread(*line, z, z_msg, z_buf, z_send, z_recv)
    ca, cb = ea - wide(ga), eb - wide(gb)
    collect(*line, kl_msg, kl_buf, kl_send, kl_recv)
    k1 = total_of(kl_buf)
    collect(*line, zx_msg, zx_buf, zx_send, zx_recv)
    acc = total_of(zx_buf)
    f_mean, ff = acc[2:4], acc[4:5]
    ga, gb = f_mean[0:1] * (1.0 / total), f_mean[1:2] * (1.0 / total)
    fix = k1[0:8] * ga + k1[8:16] * gb
    along = pieces([zx_buf[i, 0:2] for i in range(LINE)])
    ha = along[0:1] * (1.0 / total) - wide(ga) + DIAG_SHIFT * ca
    hb = along[1:2] * (1.0 / total) - wide(gb) + DIAG_SHIFT * cb
    c_tile, h_tile = fold(ca, cb), fold(ha, hb)
    collect(*line, z_msg, z_buf, z_send, z_recv)
    a_tile = total_of(z_buf) - fix

    upper = lax.broadcasted_iota(jnp.int32, (8, 128), 0) < 4

    def tile_sum(value):
        return row_sum(jnp.sum(value, axis=0, keepdims=True))

    mean_re = tile_sum(jnp.where(upper, a_tile, 0.0)) * (1.0 / block)
    mean_im = tile_sum(jnp.where(upper, 0.0, a_tile)) * (1.0 / block)
    apart = a_tile - jnp.where(upper, mean_re, mean_im)
    scalars = [
        tile_sum(c_tile * a_tile),
        tile_sum(h_tile * a_tile),
        tile_sum(apart * apart),
        mean_re,
        mean_im,
    ]
    s_msg[...] = pack_rows(scalars, 8)
    spread(*plane, w, s_msg, s_buf, s_send, s_recv)
    a_mine = piece(a_tile, z)

    for copy in w2_copies:
        copy.wait_send()

    def e_drain(d, carry):
        e_copy(d).wait_send()
        return carry

    lax.fori_loop(1, LINE * pn, e_drain, 0)
    drain(*plane, w, occ_mine.at[core], occ_plane.at[core], op_send, op_recv)
    drain(*line, z, occ_mine.at[core], occ_line.at[core], ol_send, ol_recv)
    for share in shares:
        share.wait_send()
    drain(*plane, w, kp_msg, kp_buf, kp_send, kp_recv)
    drain(*line, z, kl_msg, kl_buf, kl_send, kl_recv)
    drain(*plane, w, yx_msg, yx_buf, yx_send, yx_recv)
    drain(*plane, w, y_msg, y_buf, y_send, y_recv)
    drain(*line, z, zx_msg, zx_buf, zx_send, zx_recv)
    drain(*line, z, z_msg, z_buf, z_send, z_recv)

    collect(*plane, s_msg, s_buf, s_send, s_recv)
    s = total_of(s_buf)
    means = s * (1.0 / PLANE)
    spread_sq = jnp.square(s_buf[0] - means)
    for j in range(1, PLANE):
        spread_sq = spread_sq + jnp.square(s_buf[j] - means)
    f_af, af_af = s[0:1], s[1:2]
    centered = s[2:3] + float(block) * (spread_sq[3:4] + spread_sq[4:5])
    af_aaf = centered * (1.0 / total) + DIAG_SHIFT * af_af
    alpha0 = ff / f_af
    rr = ff - 2.0 * alpha0 * f_af + alpha0 * alpha0 * af_af
    beta = rr / ff
    near = 1.0 + beta
    curv = near * near * f_af - 2.0 * near * alpha0 * af_af + alpha0 * alpha0 * af_aaf
    alpha1 = rr / curv
    on_f = alpha0 + alpha1 * near
    on_af = alpha1 * alpha0
    out_ref[2:4] = on_f * (f_mine - f_mean) - on_af * (a_mine - means[3:5])
    drain(*plane, w, s_msg, s_buf, s_send, s_recv)


def body(occ, counts, orb, elem, step, w1, bias, w2, readout):
    samples = occ.shape[0]
    slots = orb.shape[1]
    depth, hid2 = w2.shape
    hid = w1.shape[1]
    block = LINE * samples
    vmem = pl.BlockSpec(memory_space=pltpu.VMEM)
    hbm = pl.BlockSpec(memory_space=pltpu.HBM)
    dma = pltpu.SemaphoreType.DMA
    inputs = (
        occ,
        counts.reshape(1, samples),
        orb,
        elem,
        step.reshape(1, 1),
        w1,
        bias.reshape(1, hid),
        w2,
        readout,
    )

    def message(n, height):
        return [pltpu.VMEM((height, 128), F32), pltpu.VMEM((n, height, 128), F32)]

    out = pl.pallas_call(
        kernel,
        out_shape=jax.ShapeDtypeStruct((4, 128), F32),
        in_specs=[hbm] * 9,
        out_specs=vmem,
        scratch_shapes=[
            *[pltpu.VMEM(x.shape, x.dtype) for x in inputs],
            dma((9,)),
            pltpu.VMEM((2, samples // 2, 256), BF16),
            pltpu.VMEM((2, LINE, samples // 2, 256), BF16),
            pltpu.VMEM((2, PLANE, samples // 2, 256), BF16),
            pltpu.VMEM((depth * PARAMS, hid2), BF16),
            pltpu.VMEM((slots, hid), BF16),
            pltpu.VMEM((slots, samples), BF16),
            pltpu.VMEM((samples, slots), BF16),
            pltpu.VMEM((PLANE, 2, samples // 2, hid), BF16),
            pltpu.VMEM((PLANE, 2, samples // 2, hid2), F32),
            pltpu.VMEM((3, block, block), F32),
            *[pltpu.VMEM((3, block, block), BF16)] * 4,
            *message(LINE * PARAMS, 2),
            *message(PLANE, 16),
            *message(LINE, 16),
            *message(PLANE, 4),
            *message(PLANE, 8),
            *message(LINE, 8),
            *message(LINE, 8),
            *message(PLANE, 8),
            pltpu.VMEM((8, 128), F32),
            dma((5,)),
            dma((5,)),
            *[dma((n,)) for n in (8, 8, 8, 8, 2, 2, 32, 32, *[8] * 14)],
        ],
        compiler_params=pltpu.CompilerParams(
            collective_id=0, has_side_effects=True, vmem_limit_bytes=61 * 1024 * 1024
        ),
    )(*inputs)
    return out[0:2, :samples], out[2:4, :samples]


def solution(mesh):
    return jax.shard_map(
        body,
        mesh=mesh,
        in_specs=(
            P("samples", None),
            P("samples"),
            P(None, ("samples", "params")),
            P(None, ("samples", "params")),
            P(),
            P(),
            P(),
            P("params", None),
            P(),
        ),
        out_specs=(P(None, "samples"), P(None, "samples")),
        check_vma=False,
    )
```

```python
import jax
import jax.numpy as jnp
from jax import lax
from jax.experimental import pallas as pl
from jax.experimental.pallas import tpu as pltpu
from jax.sharding import PartitionSpec as P

FIELD_SCALE = 0.8
FIELD_RATE = 0.0123
DIAG_SHIFT = 0.01
LINE = 8
PLANE = 8
PARAMS = 4
MESH = pl.DeviceIdType.MESH
F32 = jnp.float32
BF16 = jnp.bfloat16


def sincos(x):
    n = jnp.floor(x * 0.6366197723675814 + 0.5)
    r = x - n * 1.5703125
    r = r - n * 4.8351287841796875e-4
    r = r - n * 3.1385570764541626e-7
    r = r - n * 6.0771005065061922e-11
    z = r * r
    s = r + r * z * (-1.6666654611e-1 + z * (8.3321608736e-3 - z * 1.9515295891e-4))
    c = 1.0 - 0.5 * z + z * z * (
        4.166664568298827e-2 + z * (-1.388731625493765e-3 + z * 2.443315711809948e-5)
    )
    quad = n - 4.0 * jnp.floor(n * 0.25)
    odd = (quad == 1.0) | (quad == 3.0)
    sin = jnp.where(odd, c, s)
    cos = jnp.where(odd, s, c)
    sin = jnp.where(quad >= 2.0, -sin, sin)
    cos = jnp.where((quad == 1.0) | (quad == 2.0), -cos, cos)
    return sin, cos


def parts3(x):
    hi = x.astype(BF16).astype(F32)
    rest = x - hi
    mid = rest.astype(BF16).astype(F32)
    return hi, mid, rest - mid


def pack_rows(rows, height):
    width = rows[0].shape[1]
    place = lax.broadcasted_iota(jnp.int32, (height, width), 0)
    out = jnp.zeros((height, width), F32)
    for i, row in enumerate(rows):
        out = jnp.where(place == i, jnp.broadcast_to(row, (height, width)), out)
    return out


def nn(a, b):
    return lax.dot_general(a, b, (((1,), (0,)), ((), ())), preferred_element_type=F32)


def nt(a, b):
    return lax.dot_general(a, b, (((1,), (1,)), ((), ())), preferred_element_type=F32)


def tn(a, b):
    return lax.dot_general(a, b, (((0,), (0,)), ((), ())), preferred_element_type=F32)


def kernel(
    occ_hbm,
    counts_hbm,
    orb_hbm,
    elem_hbm,
    step_hbm,
    w1_hbm,
    bias_hbm,
    w2_hbm,
    readout_hbm,
    out_ref,
    occ_ref,
    counts_ref,
    orb_ref,
    elem_ref,
    step_ref,
    w1_ref,
    bias_ref,
    w2_ref,
    readout_ref,
    in_sem,
    occ_mine,
    occ_line,
    occ_plane,
    w2_full,
    slot_hid,
    pick,
    pick_t,
    hid_plane,
    slope_plane,
    kt_full,
    kt_hi,
    kt_lo,
    kr_hi,
    kr_lo,
    e_msg,
    e_buf,
    kp_msg,
    kp_buf,
    kl_msg,
    kl_buf,
    yx_msg,
    yx_buf,
    y_msg,
    y_buf,
    zx_msg,
    zx_buf,
    z_msg,
    z_buf,
    s_msg,
    s_buf,
    own_buf,
    w2_send,
    w2_recv,
    op_send,
    op_recv,
    ol_send,
    ol_recv,
    share_send,
    share_recv,
    e_send,
    e_recv,
    kp_send,
    kp_recv,
    kl_send,
    kl_recv,
    yx_send,
    yx_recv,
    y_send,
    y_recv,
    zx_send,
    zx_recv,
    z_send,
    z_recv,
    s_send,
    s_recv,
):
    outside = (occ_hbm, w2_hbm, w1_hbm, orb_hbm, counts_hbm, bias_hbm, elem_hbm, step_hbm, readout_hbm)
    inside = (occ_ref, w2_ref, w1_ref, orb_ref, counts_ref, bias_ref, elem_ref, step_ref, readout_ref)
    loads = [pltpu.make_async_copy(a, c, in_sem.at[i]) for i, (a, c) in enumerate(zip(outside, inside))]
    samples, orbitals = occ_ref.shape
    slots = orb_ref.shape[1]
    depth = w2_ref.shape[0]
    pn = PARAMS
    block = LINE * samples
    total = float(block * PLANE)

    b = lax.axis_index("samples")
    p = lax.axis_index("params")
    z = b // PLANE
    w = b % PLANE
    p_core = p + 1 - 2 * (p % 2)
    p_far = p + 2 - 4 * (p // 2)
    p_cross = p_far + 1 - 2 * (p_far % 2)
    b_pair = b + 1 - 2 * (b % 2)

    def line_peer(d):
        to = lax.rem(z + d, LINE)
        return to, (to * PLANE + w, p)

    def plane_peer(d):
        y, half = w // 2, w % 2
        to_y = lax.rem(y + d // 2, PLANE // 2)
        if d % 2:
            to = to_y * 2 + 1 - half
            return to, (z * PLANE + to, p_far)
        to = to_y * 2 + half
        return to, (z * PLANE + to, p)

    LINE_ORDER = (4, 3, 5, 2, 6, 1, 7)
    PLANE_ORDER = (5, 4, 3, 7, 2, 6, 1)

    def energy_peer(d):
        return lax.rem(z + d // pn, LINE) * PLANE + w, lax.rem(p + lax.rem(d, pn), pn)

    def copy_to(src, dst, send, recv, device):
        return pltpu.make_async_remote_copy(
            src_ref=src, dst_ref=dst, send_sem=send, recv_sem=recv, device_id=device, device_id_type=MESH
        )

    def spread(peer, order, me, msg, buf, send, recv, keep=True):
        for d in order:
            copy_to(msg, buf.at[me], send.at[d], recv.at[me], peer(d)[1]).start()
        if keep:
            buf[me] = msg[...]

    def collect(peer, order, msg, buf, send, recv):
        for d in reversed(order):
            place, device = peer(d)
            copy_to(msg, buf.at[place], send.at[d], recv.at[place], device).wait_recv()

    def drain(peer, order, me, msg, buf, send, recv):
        for d in order:
            copy_to(msg, buf.at[me], send.at[d], recv.at[me], peer(d)[1]).wait_send()

    line = (line_peer, LINE_ORDER)
    plane = (plane_peer, PLANE_ORDER)

    barrier = pltpu.get_barrier_semaphore()

    def signal(device):
        pl.semaphore_signal(barrier, inc=1, device_id=device, device_id_type=MESH)

    signal((b_pair, p_cross))
    for d in PLANE_ORDER:
        signal(plane_peer(d)[1])

    for dz in (0, *LINE_ORDER):
        to_b = lax.rem(z + dz, LINE) * PLANE + w
        for dp in range(pn):
            if dz or dp:
                signal((to_b, lax.rem(p + dp, pn)))
    for load in loads:
        load.start()

    loads[0].wait()
    occ = occ_ref[...].astype(F32)
    occ_mine[...] = jnp.zeros_like(occ_mine)
    core = p % 2
    rows_here = samples // 2
    for h in range(2):
        occ_mine[h, :, :orbitals] = occ[h * rows_here : (h + 1) * rows_here].astype(BF16)
    pl.semaphore_wait(barrier, LINE * pn - 1 + PLANE - 1 + 1)

    half = depth // 2
    whole = pl.ds(pl.multiple_of(p * depth, depth), depth)
    w2_copies = []
    for d, far in ((0, p_far), (1, p_cross)):
        for h, to in ((0, b), (1, b_pair)):
            rows = pl.ds(pl.multiple_of(p * depth + h * half, half), half)
            i = 1 + d * 2 + h
            w2_copies.append(
                copy_to(w2_hbm.at[pl.ds(h * half, half)], w2_full.at[rows], w2_send.at[i], w2_recv.at[i], (to, far))
            )
    w2_copies.append(copy_to(w2_hbm, w2_full.at[whole], w2_send.at[0], w2_recv.at[0], (b, p_core)))
    for copy in w2_copies:
        copy.start()

    spread(*plane, w, occ_mine.at[core], occ_plane.at[core], op_send, op_recv, False)
    spread(*line, z, occ_mine.at[core], occ_line.at[core], ol_send, ol_recv, False)
    occ_line[core, z] = occ_mine[core]
    occ_plane[core, w] = occ_mine[core]
    loads[1].wait()
    w2_full[whole] = w2_ref[...]

    for load in loads[2:]:
        load.wait()
    counts = jnp.broadcast_to(counts_ref[...].astype(F32), (8, samples))
    r_id = lax.broadcasted_iota(jnp.int32, (samples, samples), 0)
    c_id = lax.broadcasted_iota(jnp.int32, (samples, samples), 1)
    upto = (r_id <= c_id).astype(BF16)
    c_hi, c_mid, c_lo = parts3(counts)
    ends = nn(c_hi.astype(BF16), upto) + nn(c_mid.astype(BF16), upto) + nn(c_lo.astype(BF16), upto)
    begins = ends - counts
    position = (p + pn * lax.broadcasted_iota(jnp.int32, (slots, samples), 0)).astype(F32)
    pick[...] = ((begins[0:1] <= position) & (position < ends[0:1])).astype(BF16)
    ends_col, begins_col = ends.T[:, 0:1], begins.T[:, 0:1]
    position = (p + pn * lax.broadcasted_iota(jnp.int32, (samples, slots), 1)).astype(F32)
    pick_t[...] = ((begins_col <= position) & (position < ends_col)).astype(BF16)
    ends = ends[0:1]
    occ_t = occ.T.astype(BF16)
    w1 = w1_ref[...]
    bias = bias_ref[...]
    chunk = 256
    for start_row in range(0, slots, chunk):
        rows = slice(start_row, start_row + chunk)
        base = nn(occ_t, pick_t[:, rows])
        column = lax.broadcasted_iota(jnp.int32, (orbitals, chunk), 0)
        orb = orb_ref[:, rows]
        flip = orb[0:1] == column
        for u in range(1, orb_ref.shape[0]):
            flip = flip | (orb[u : u + 1] == column)
        flipped = jnp.where(flip, 1.0 - base, base).astype(BF16)
        slot_hid[rows] = jnp.tanh(tn(flipped, w1) + bias).astype(BF16)
    hidden = jnp.tanh(nn(occ.astype(BF16), w1) + bias).astype(BF16)

    readout = readout_ref[...]
    r_rows = pack_rows([x[i : i + 1] for x in parts3(readout) for i in range(2)], 128)
    r_cols = r_rows.T.astype(BF16)
    angle = jnp.broadcast_to(step_ref[...].astype(F32), (1, slots)) * FIELD_RATE
    field = FIELD_SCALE * sincos(angle)[0]
    elem = elem_ref[...]
    weight = elem[0:1] + field * elem[1:2]
    slot_at = (p + pn * lax.broadcasted_iota(jnp.int32, (1, slots), 1)).astype(F32)
    used = slot_at < ends[0:1, samples - 1 : samples]
    for copy in w2_copies:
        copy.wait_recv()
    w2 = w2_full[...]
    shares = [
        copy_to(buf.at[core], buf.at[core], share_send.at[i], share_recv.at[i], (b, p_core))
        for i, buf in enumerate((occ_line, occ_plane))
    ]
    collect(*line, occ_mine.at[core], occ_line.at[core], ol_send, ol_recv)
    shares[0].start()

    def logs_of(hid):
        mid = jnp.tanh(nn(hid, w2))
        hi = mid.astype(BF16)
        lo = (mid - hi.astype(F32)).astype(BF16)
        out = (nn(hi, r_cols) + nn(lo, r_cols)).T
        return out[0:2] + out[2:4] + out[4:6]

    logs = logs_of(hidden)
    slot_logs = logs_of(slot_hid[...])
    l_rows = pack_rows([x[i : i + 1] for x in parts3(logs) for i in range(2)], 16).astype(BF16)
    parent_logs = nn(l_rows, pick_t[...])
    parent_logs = parent_logs[0:2] + parent_logs[2:4] + parent_logs[4:6]
    diff = slot_logs - parent_logs
    size = jnp.exp(diff[0:1])
    sin, cos = sincos(diff[1:2])
    contrib = [jnp.where(used, weight * (size * cos), 0.0), jnp.where(used, weight * (size * sin), 0.0)]
    splits = [parts3(x) for x in contrib]
    e_rows = pack_rows([splits[i][j] for j in range(3) for i in range(2)], 16).astype(BF16)
    energy = nn(e_rows, pick[...])
    energy = energy[0:2] + energy[2:4] + energy[4:6]
    e_msg[...] = jnp.concatenate([energy, jnp.zeros((2, 128 - samples), F32)], axis=1)

    me = z * pn + p

    def e_copy(d):
        return copy_to(e_msg, e_buf.at[me], e_send.at[d], e_recv.at[me], energy_peer(d))

    for dz in (*LINE_ORDER, 0):
        for dp in range(pn):
            if dz * pn + dp:
                e_copy(dz * pn + dp).start()
    e_buf[me] = e_msg[...]

    def fold(re, im):
        return pack_rows([row[:, i * 128 : (i + 1) * 128] for row in (re, im) for i in range(block // 128)], 8)

    def unfold(tile):
        n = block // 128
        return [jnp.concatenate([tile[at + i : at + i + 1] for i in range(n)], axis=1) for at in (0, n)]

    def wide(row):
        return jnp.concatenate([row] * (block // 128), axis=1)

    def row_sum(value):
        return jnp.broadcast_to(jnp.sum(value, axis=1, keepdims=True), (1, 128))

    def hidden_of(parts):
        rows = jnp.concatenate(parts, axis=0)[:, :orbitals]
        return jnp.tanh(nn(rows, w1) + bias).astype(BF16)

    def slope_of(hid):
        mid = jnp.tanh(nn(hid, w2))
        return 1.0 - mid * mid

    def half_of_plane(h):
        hid = hidden_of([occ_plane[h, i] for i in range(PLANE)])
        slope = slope_of(hid)
        for i in range(PLANE):
            rows = slice(i * rows_here, (i + 1) * rows_here)
            hid_plane[i, h] = hid[rows]
            slope_plane[i, h] = slope[rows]

    collect(*plane, occ_mine.at[core], occ_plane.at[core], op_send, op_recv)
    shares[1].start()
    shares[0].wait_recv()
    hid_c = hidden_of([occ_line[h, i] for i in range(LINE) for h in range(2)])
    slope_c = slope_of(hid_c)
    half_of_plane(core)
    shares[1].wait_recv()
    half_of_plane(1 - core)
    hid_r = hid_plane[...].reshape(block, hid_plane.shape[3])
    slope_r = slope_plane[...].reshape(block, slope_plane.shape[3])
    gram = nt(hid_c, hid_r)
    r_hi = slope_r.astype(BF16)
    r_lo = (slope_r - r_hi.astype(F32)).astype(BF16)
    ones_r, ones_c = [], []
    pairs = (readout[0:1] * readout[0:1], readout[0:1] * readout[1:2], readout[1:2] * readout[1:2])
    for t, pair in enumerate(pairs):
        scaled = slope_c * pair
        s_hi = scaled.astype(BF16)
        s_lo = (scaled - s_hi.astype(F32)).astype(BF16)
        kt = gram * (nt(s_hi, r_hi) + (nt(s_lo, r_hi) + nt(s_hi, r_lo)))
        hi = kt.astype(BF16)
        lo = (kt - hi.astype(F32)).astype(BF16)
        kt_hi[t] = hi
        kt_lo[t] = lo
        kt_full[t] = kt
        ones_r.append(jnp.sum(kt, axis=0, keepdims=True))
    kp_msg[0:8] = fold(ones_r[0], ones_r[1])
    kp_msg[8:16] = fold(ones_r[1], ones_r[2])
    spread(*plane, w, kp_msg, kp_buf, kp_send, kp_recv)

    def apply(va, vb, ones, k_hi, k_lo):
        ma = jnp.sum(va, axis=1, keepdims=True) * (1.0 / block)
        mb = jnp.sum(vb, axis=1, keepdims=True) * (1.0 / block)
        rows = pack_rows([*parts3(va - ma), *parts3(vb - mb)], 16).astype(BF16)
        outs = []
        for t in range(3):
            out = nn(rows, k_hi[t]) + nn(rows, k_lo[t])
            outs.append((out[0:1] + out[1:2] + out[2:3], out[3:4] + out[4:5] + out[5:6]))
        y_re = outs[0][0] + outs[1][1] + (ones[0] * ma + ones[1] * mb)
        y_im = outs[1][0] + outs[2][1] + (ones[1] * ma + ones[2] * mb)
        return y_re, y_im

    def total_of(buf):
        acc = buf[0]
        for j in range(1, buf.shape[0]):
            acc = acc + buf[j]
        return acc

    def pieces(tiles):
        pairs = [tiles[i] + pltpu.roll(tiles[i + 1], samples, 1) for i in range(0, len(tiles), 2)]
        return jnp.concatenate(pairs, axis=1)

    lane = lax.broadcasted_iota(jnp.int32, (2, 128), 1)

    def piece(tile, place):
        own_buf[...] = tile
        rows = jnp.concatenate([own_buf[pl.ds(place // 2, 1)], own_buf[pl.ds(place // 2 + 4, 1)]], axis=0)
        odd = jnp.full(rows.shape, place % 2, jnp.int32) == 1
        rows = jnp.where(odd, pltpu.roll(rows, samples, 1), rows)
        return jnp.where(lane < samples, rows, 0.0)

    for dz in (0, *reversed(LINE_ORDER)):
        to_z = lax.rem(z + dz, LINE)
        for dp in range(pn):
            if dz or dp:
                to_p = lax.rem(p + dp, pn)
                place = to_z * pn + to_p
                d = dz * pn + dp
                copy_to(
                    e_msg, e_buf.at[place], e_send.at[d], e_recv.at[place], (to_z * PLANE + w, to_p)
                ).wait_recv()

    def over_params(i):
        acc = e_buf[i * pn]
        for j in range(1, pn):
            acc = acc + e_buf[i * pn + j]
        return acc

    energies = pieces([over_params(i) for i in range(LINE)])
    mine = over_params(z)
    out_ref[0:2] = mine

    ea = energies[1:2] * (1.0 / total)
    eb = energies[0:1] * (-1.0 / total)
    yx_msg[0:2] = mine
    yx_msg[2:3] = row_sum(ea) * (1.0 / total)
    yx_msg[3:4] = row_sum(eb) * (1.0 / total)
    spread(*plane, w, yx_msg, yx_buf, yx_send, yx_recv)
    y_msg[...] = fold(*apply(ea, eb, ones_r, kt_hi, kt_lo))
    spread(*plane, w, y_msg, y_buf, y_send, y_recv)
    for t in range(3):
        turned = kt_full[t].T
        hi = turned.astype(BF16)
        kr_hi[t] = hi
        kr_lo[t] = (turned - hi.astype(F32)).astype(BF16)
        ones_c.append(jnp.sum(turned, axis=0, keepdims=True))
    kl_msg[0:8] = fold(ones_c[0], ones_c[1])
    kl_msg[8:16] = fold(ones_c[1], ones_c[2])
    spread(*line, z, kl_msg, kl_buf, kl_send, kl_recv)
    collect(*plane, kp_msg, kp_buf, kp_send, kp_recv)
    k1 = total_of(kp_buf)
    collect(*plane, yx_msg, yx_buf, yx_send, yx_recv)
    means = total_of(yx_buf)
    ga, gb = means[2:3], means[3:4]
    around = pieces([yx_buf[i] for i in range(PLANE)])
    fa = around[1:2] * (1.0 / total) - wide(ga)
    fb = around[0:1] * (-1.0 / total) - wide(gb)
    fix = k1[0:8] * ga + k1[8:16] * gb
    collect(*plane, y_msg, y_buf, y_send, y_recv)
    f_tile = total_of(y_buf) - fix
    f_re, f_im = unfold(f_tile)

    f_mine = piece(f_tile, w)
    zx_msg[0:2] = f_mine
    zx_msg[2:3] = row_sum(f_re) * (1.0 / total)
    zx_msg[3:4] = row_sum(f_im) * (1.0 / total)
    zx_msg[4:5] = row_sum(fa * f_re + fb * f_im)
    zx_msg[5:8] = jnp.zeros((3, 128), F32)
    spread(*line, z, zx_msg, zx_buf, zx_send, zx_recv)
    ha = f_re * (1.0 / total) + DIAG_SHIFT * fa
    hb = f_im * (1.0 / total) + DIAG_SHIFT * fb
    z_msg[...] = fold(*apply(ha, hb, ones_c, kr_hi, kr_lo))
    spread(*line, z, z_msg, z_buf, z_send, z_recv)
    ca, cb = ea - wide(ga), eb - wide(gb)
    collect(*line, kl_msg, kl_buf, kl_send, kl_recv)
    k1 = total_of(kl_buf)
    collect(*line, zx_msg, zx_buf, zx_send, zx_recv)
    acc = total_of(zx_buf)
    f_mean, ff = acc[2:4], acc[4:5]
    ga, gb = f_mean[0:1] * (1.0 / total), f_mean[1:2] * (1.0 / total)
    fix = k1[0:8] * ga + k1[8:16] * gb
    along = pieces([zx_buf[i, 0:2] for i in range(LINE)])
    ha = along[0:1] * (1.0 / total) - wide(ga) + DIAG_SHIFT * ca
    hb = along[1:2] * (1.0 / total) - wide(gb) + DIAG_SHIFT * cb
    c_tile, h_tile = fold(ca, cb), fold(ha, hb)
    collect(*line, z_msg, z_buf, z_send, z_recv)
    a_tile = total_of(z_buf) - fix

    upper = lax.broadcasted_iota(jnp.int32, (8, 128), 0) < 4

    def tile_sum(value):
        return row_sum(jnp.sum(value, axis=0, keepdims=True))

    mean_re = tile_sum(jnp.where(upper, a_tile, 0.0)) * (1.0 / block)
    mean_im = tile_sum(jnp.where(upper, 0.0, a_tile)) * (1.0 / block)
    apart = a_tile - jnp.where(upper, mean_re, mean_im)
    scalars = [
        tile_sum(c_tile * a_tile),
        tile_sum(h_tile * a_tile),
        tile_sum(apart * apart),
        mean_re,
        mean_im,
    ]
    s_msg[...] = pack_rows(scalars, 8)
    spread(*plane, w, s_msg, s_buf, s_send, s_recv)
    a_mine = piece(a_tile, z)

    for copy in w2_copies:
        copy.wait_send()

    def e_drain(d, carry):
        e_copy(d).wait_send()
        return carry

    lax.fori_loop(1, LINE * pn, e_drain, 0)
    drain(*plane, w, occ_mine.at[core], occ_plane.at[core], op_send, op_recv)
    drain(*line, z, occ_mine.at[core], occ_line.at[core], ol_send, ol_recv)
    for share in shares:
        share.wait_send()
    drain(*plane, w, kp_msg, kp_buf, kp_send, kp_recv)
    drain(*line, z, kl_msg, kl_buf, kl_send, kl_recv)
    drain(*plane, w, yx_msg, yx_buf, yx_send, yx_recv)
    drain(*plane, w, y_msg, y_buf, y_send, y_recv)
    drain(*line, z, zx_msg, zx_buf, zx_send, zx_recv)
    drain(*line, z, z_msg, z_buf, z_send, z_recv)

    collect(*plane, s_msg, s_buf, s_send, s_recv)
    s = total_of(s_buf)
    means = s * (1.0 / PLANE)
    spread_sq = jnp.square(s_buf[0] - means)
    for j in range(1, PLANE):
        spread_sq = spread_sq + jnp.square(s_buf[j] - means)
    f_af, af_af = s[0:1], s[1:2]
    centered = s[2:3] + float(block) * (spread_sq[3:4] + spread_sq[4:5])
    af_aaf = centered * (1.0 / total) + DIAG_SHIFT * af_af
    alpha0 = ff / f_af
    rr = ff - 2.0 * alpha0 * f_af + alpha0 * alpha0 * af_af
    beta = rr / ff
    near = 1.0 + beta
    curv = near * near * f_af - 2.0 * near * alpha0 * af_af + alpha0 * alpha0 * af_aaf
    alpha1 = rr / curv
    on_f = alpha0 + alpha1 * near
    on_af = alpha1 * alpha0
    out_ref[2:4] = on_f * (f_mine - f_mean) - on_af * (a_mine - means[3:5])
    drain(*plane, w, s_msg, s_buf, s_send, s_recv)


def body(occ, counts, orb, elem, step, w1, bias, w2, readout):
    samples = occ.shape[0]
    slots = orb.shape[1]
    depth, hid2 = w2.shape
    hid = w1.shape[1]
    block = LINE * samples
    vmem = pl.BlockSpec(memory_space=pltpu.VMEM)
    hbm = pl.BlockSpec(memory_space=pltpu.HBM)
    dma = pltpu.SemaphoreType.DMA
    inputs = (
        occ,
        counts.reshape(1, samples),
        orb,
        elem,
        step.reshape(1, 1),
        w1,
        bias.reshape(1, hid),
        w2,
        readout,
    )

    def message(n, height):
        return [pltpu.VMEM((height, 128), F32), pltpu.VMEM((n, height, 128), F32)]

    out = pl.pallas_call(
        kernel,
        out_shape=jax.ShapeDtypeStruct((4, 128), F32),
        in_specs=[hbm] * 9,
        out_specs=vmem,
        scratch_shapes=[
            *[pltpu.VMEM(x.shape, x.dtype) for x in inputs],
            dma((9,)),
            pltpu.VMEM((2, samples // 2, 256), BF16),
            pltpu.VMEM((2, LINE, samples // 2, 256), BF16),
            pltpu.VMEM((2, PLANE, samples // 2, 256), BF16),
            pltpu.VMEM((depth * PARAMS, hid2), BF16),
            pltpu.VMEM((slots, hid), BF16),
            pltpu.VMEM((slots, samples), BF16),
            pltpu.VMEM((samples, slots), BF16),
            pltpu.VMEM((PLANE, 2, samples // 2, hid), BF16),
            pltpu.VMEM((PLANE, 2, samples // 2, hid2), F32),
            pltpu.VMEM((3, block, block), F32),
            *[pltpu.VMEM((3, block, block), BF16)] * 4,
            *message(LINE * PARAMS, 2),
            *message(PLANE, 16),
            *message(LINE, 16),
            *message(PLANE, 4),
            *message(PLANE, 8),
            *message(LINE, 8),
            *message(LINE, 8),
            *message(PLANE, 8),
            pltpu.VMEM((8, 128), F32),
            dma((5,)),
            dma((5,)),
            *[dma((n,)) for n in (8, 8, 8, 8, 2, 2, 32, 32, *[8] * 14)],
        ],
        compiler_params=pltpu.CompilerParams(
            collective_id=0, has_side_effects=True, vmem_limit_bytes=61 * 1024 * 1024
        ),
    )(*inputs)
    return out[0:2, :samples], out[2:4, :samples]


def solution(mesh):
    return jax.shard_map(
        body,
        mesh=mesh,
        in_specs=(
            P("samples", None),
            P("samples"),
            P(None, ("samples", "params")),
            P(None, ("samples", "params")),
            P(),
            P(),
            P(),
            P("params", None),
            P(),
        ),
        out_specs=(P(None, "samples"), P(None, "samples")),
        check_vma=False,
    )
```
